32 devices in a mesh: dp: 16 (over z, y, x), tensor: 2 (over core).
Axes of the slice: x: 2, y: 2, z: 4, core: 2. Of those that a mesh axis runs over, the one named last changes fastest.
Arguments:
- residual: bfloat16 [16384, 1024], P(('dp', 'tensor')), may hold values from -6 to 6
- norm1_gain: float32 [1024], replicated, may hold values from 0.5 to 1.5
- norm1_bias: float32 [1024], replicated, may hold values from -3 to 3
- norm2_gain: float32 [1024], replicated, may hold values from 0.5 to 1.5
- norm2_bias: float32 [1024], replicated, may hold values from -3 to 3
- qkv_weight: bfloat16 [1024, 3, 1024], P(None, None, 'tensor'), may hold values from -2 to 2, as said below
- qkv_bias: float32 [3, 1024], P(None, 'tensor'), may hold values from -3 to 3
- dense_weight: bfloat16 [1024, 1024], P('tensor'), may hold values from -0.75 to 0.75
- inner_weight: bfloat16 [1024, 4096], P(None, 'tensor'), may hold values from -0.1875 to 0.1875
- inner_bias: float32 [4096], P('tensor'), may hold values from -3 to 3
- outer_weight: bfloat16 [4096, 1024], P('tensor'), may hold values from -0.09375 to 0.09375
- out_bias: float32 [1024], replicated, may hold values from -3 to 3
- cotangent: bfloat16 [16384, 1024], P(('dp', 'tensor')), may hold values from -6 to 6
- seq_lengths: int32 [16, 4], P('dp'), may hold values from 0 to 512, as said below
Outputs:
- layer_out: bfloat16 [16384, 1024], P(('dp', 'tensor'))
- residual_grad: bfloat16 [16384, 1024], P(('dp', 'tensor'))
- gain1_grad: float32 [1024], replicated
- bias1_grad: float32 [1024], replicated
- gain2_grad: float32 [1024], replicated
- bias2_grad: float32 [1024], replicated
- qkv_grad: float32 [1024, 3, 1024], P(None, None, 'tensor')
- qkvbias_grad: float32 [3, 1024], P(None, 'tensor')
- dense_grad: float32 [1024, 1024], P('tensor')
- inner_grad: float32 [1024, 4096], P(None, 'tensor')
- innerbias_grad: float32 [4096], P('tensor')
- outer_grad: float32 [4096, 1024], P('tensor')
- outbias_grad: float32 [1024], replicated
The draws below stay inside these ranges and needn't reach their ends.
Inputs may be any that keep to these rules, and one draw needn't show every extreme that they name: `seq_lengths`: row r lists the lengths of the sequences packed into index r of dp in order, zero for an unused slot; each row sums to at most 1024. In every draw some row holds two sequences of 512 rows and is full. `qkv_weight`: entries are independent.
All inputs are finite; a program needn't handle non-finite values.
Results may differ from the reference program's by a relative error of at most 0.0085.
Values may be sent and summed in bfloat16 or wider, within the bound.
No kernel may reach another device: no remote copies, remote signals or barrier semaphores. Data moves between devices by JAX's collectives and lax.ppermute only.
A program may use at most 256 MiB of HBM per device.

```python
import math
import jax
import jax.numpy as jnp
from jax import lax

D = 1024
HEADS = 16
FF = 4096
HD = 64
ROT = 16
CAP = 1024
MAXLEN = 512
SLOTS = 4
TOKENS = 16384
N_DP = 16
N_TENSOR = 2


def draw_seq_lengths(key, part):
    first_key, second_key, third_key = jax.random.split(key, 3)
    raw_lengths = jax.random.randint(first_key, (N_DP, SLOTS), 1, MAXLEN + 1)
    used_slots = jax.random.randint(second_key, (N_DP, 1), 1, SLOTS + 1)
    slot_index = jnp.arange(SLOTS, dtype=jnp.int32)[None, :]
    raw_lengths = jnp.where(slot_index < used_slots, raw_lengths, 0)
    full_rank = jax.random.randint(third_key, (), 0, N_DP)
    rank_index = jnp.arange(N_DP, dtype=jnp.int32)[:, None]
    raw_lengths = jnp.where(rank_index == full_rank, jnp.where(slot_index < 2, MAXLEN, 0), raw_lengths)
    before = jnp.cumsum(raw_lengths, axis=1) - raw_lengths
    lengths = jnp.clip(jnp.minimum(raw_lengths, CAP - before), 0, MAXLEN)
    return lengths.astype(jnp.int32)


def draw_qkv_weight(key, part):
    first_key = jax.random.fold_in(key, 0)
    standard = jnp.clip(jax.random.normal(first_key, (D, 3, HEADS * HD), jnp.float32), -3.5, 3.5)
    return (standard * D ** (-0.5)).astype(jnp.bfloat16)


def block_scale(own_key, dims, pieces, smallest, largest):
    factor_of = 1.0
    for dim, parts in pieces:
        heights = jax.random.uniform(jax.random.fold_in(jax.random.fold_in(own_key, 6), dim), (parts,), jnp.float32, smallest / len(pieces), largest / len(pieces))
        factor_of = factor_of * jnp.repeat(jnp.exp(heights), dims[dim] // parts).reshape((-1,) + (1,) * (len(dims) - 1 - dim))
    return factor_of


def noise(stream_key, shape, deviation, reach, cuts=(), kind=jnp.bfloat16):
    factor_of = block_scale(stream_key, shape, cuts, -0.22, 0.18) if cuts else 1.0
    result = jax.random.normal(stream_key, shape, jnp.float32) * deviation * factor_of
    return jnp.minimum(jnp.maximum(result, -reach), reach).astype(kind)


def setup_inputs(seed: int = 0) -> dict:
    key_list = jax.random.split(jax.random.key(seed), 15)
    residual = noise(key_list[0], (TOKENS, D), 1.0, 6.0, ((0, 32),))
    norm1_gain = jnp.clip(1.0 + 0.1 * jax.random.normal(key_list[1], (D,), jnp.float32), 0.5, 1.5)
    norm1_bias = noise(key_list[2], (D,), 0.3, 3.0, (), jnp.float32)
    norm2_gain = jnp.clip(1.0 + 0.1 * jax.random.normal(key_list[3], (D,), jnp.float32), 0.5, 1.5)
    norm2_bias = noise(key_list[4], (D,), 0.3, 3.0, (), jnp.float32)
    qkv_weight = draw_qkv_weight(jax.random.fold_in(key_list[14], 71), 0)
    qkv_bias = noise(key_list[6], (3, HEADS * HD), 0.3, 3.0, ((1, 2),), jnp.float32)
    dense_weight = noise(key_list[7], (HEADS * HD, D), HD ** -0.5, 0.75, ((0, 2),))
    inner_weight = noise(key_list[8], (D, FF), D ** -0.5, 0.1875, ((1, 2),))
    inner_bias = noise(key_list[9], (FF,), 0.5, 3.0, ((0, 2),), jnp.float32)
    outer_weight = noise(key_list[10], (FF, D), FF ** -0.5, 0.09375, ((0, 2),))
    out_bias = noise(key_list[11], (D,), 0.5, 3.0, (), jnp.float32)
    cotangent = noise(key_list[12], (TOKENS, D), 1.0, 6.0, ((0, 32),))
    seq_lengths = draw_seq_lengths(jax.random.fold_in(key_list[14], 71), 0)
    return {"residual": residual, "norm1_gain": norm1_gain, "norm1_bias": norm1_bias, "norm2_gain": norm2_gain, "norm2_bias": norm2_bias, "qkv_weight": qkv_weight, "qkv_bias": qkv_bias, "dense_weight": dense_weight, "inner_weight": inner_weight, "inner_bias": inner_bias, "outer_weight": outer_weight, "out_bias": out_bias, "cotangent": cotangent, "seq_lengths": seq_lengths}


EPSILON = 1e-05
MASKED_SCORE = -1e+30
SQRT_HALF = 0.7071067811865476
INV_ROOT_TWO_PI = 0.3989422804014327

def normalize(values):
    mean_val = lax.optimization_barrier(jnp.mean(values, axis=-1, keepdims=True))
    centred = values - mean_val
    inv_std = lax.rsqrt(lax.optimization_barrier(jnp.mean(centred * centred, axis=-1, keepdims=True)) + EPSILON)
    return (centred * inv_std, inv_std)

def norm_back(upstream, normed, inv_std, gain):
    scaled = upstream * gain
    return inv_std * (scaled - lax.optimization_barrier(jnp.mean(scaled, axis=-1, keepdims=True)) - normed * lax.optimization_barrier(jnp.mean(scaled * normed, axis=-1, keepdims=True)))

def gelu_slope(preact):
    return 0.5 * (1.0 + lax.erf(preact * SQRT_HALF)) + preact * jnp.exp(-0.5 * preact * preact) * INV_ROOT_TWO_PI

def layout(lengths, row_count):
    slot_count = lengths.shape[0]
    places = jnp.arange(row_count, dtype=jnp.int32)
    seq_ends = jnp.cumsum(lengths).astype(jnp.int32)
    seq_starts = (seq_ends - lengths).astype(jnp.int32)
    segment = lax.optimization_barrier(jnp.sum((places[:, None] >= seq_ends[None, :]).astype(jnp.int32), axis=1)).astype(jnp.int32)
    member = segment[:, None] == jnp.arange(slot_count, dtype=jnp.int32)[None, :]
    position = (places - lax.optimization_barrier(jnp.sum(jnp.where(member, seq_starts[None, :], 0), axis=1))).astype(jnp.int32)
    return (segment, position)

def angles(position):
    half_rot = ROT // 2
    frequency = jnp.exp(-(2.0 * jnp.arange(half_rot, dtype=jnp.float32) / ROT) * math.log(10000.0))
    angle_table = position.astype(jnp.float32)[:, None] * frequency[None, :]
    return (jnp.cos(angle_table), jnp.sin(angle_table))

def rotate(values, cosine, sine_table):
    half_rot = ROT // 2
    lower = values[..., :half_rot]
    upper = values[..., half_rot:ROT]
    cos_grid = cosine[:, None, :]
    sin_grid = sine_table[:, None, :]
    return jnp.concatenate([lower * cos_grid - upper * sin_grid, upper * cos_grid + lower * sin_grid, values[..., ROT:]], axis=-1)

def unrotate(values, cosine, sine_table):
    half_rot = ROT // 2
    lower = values[..., :half_rot]
    upper = values[..., half_rot:ROT]
    cos_grid = cosine[:, None, :]
    sin_grid = sine_table[:, None, :]
    return jnp.concatenate([lower * cos_grid + upper * sin_grid, upper * cos_grid - lower * sin_grid, values[..., ROT:]], axis=-1)

def reference(residual, norm1_gain, norm1_bias, norm2_gain, norm2_bias, qkv_weight, qkv_bias, dense_weight, inner_weight, inner_bias, outer_weight, out_bias, cotangent, seq_lengths):
    feature_width = residual.shape[1]
    qkv_flat = qkv_weight.reshape(feature_width, -1)
    score_scale = HD ** (-0.5)
    head_width = HEADS * HD

    def one_rank(carry, inputs):
        rank_rows, rank_cot, lengths = inputs
        segment, position = layout(lengths, CAP)
        cosine, sine_table = angles(position)
        normed, inv_std = normalize(rank_rows.astype(jnp.float32))
        first_in = (normed * norm1_gain + norm1_bias).astype(jnp.bfloat16)
        second_in = (normed * norm2_gain + norm2_bias).astype(jnp.bfloat16)
        projected = (jnp.dot(first_in, qkv_flat, preferred_element_type=jnp.float32) + qkv_bias.reshape(-1)).reshape(CAP, 3, HEADS, HD)
        queries = rotate(projected[:, 0], cosine, sine_table).astype(jnp.bfloat16)
        keys_bf = rotate(projected[:, 1], cosine, sine_table).astype(jnp.bfloat16)
        values_bf = projected[:, 2].astype(jnp.bfloat16)
        columns = jnp.arange(CAP, dtype=jnp.int32)
        allowed = (segment[:, None] == segment[None, :]) & (columns[None, :] <= columns[:, None]) & (segment[:, None] < SLOTS) | (columns[None, :] == columns[:, None])
        scores = jnp.einsum('qhd,khd->hqk', queries.astype(jnp.float32), keys_bf.astype(jnp.float32)) * score_scale
        scores = jnp.where(allowed[None], scores, MASKED_SCORE)
        highest = lax.optimization_barrier(jnp.max(scores, axis=-1, keepdims=True))
        exponent = jnp.exp(scores - highest)
        row_total = lax.optimization_barrier(jnp.sum(exponent, axis=-1, keepdims=True))
        probs_bf = (exponent / row_total).astype(jnp.bfloat16)
        logsum = highest + jnp.log(row_total)
        context = jnp.einsum('hqk,khd->qhd', probs_bf.astype(jnp.float32), values_bf.astype(jnp.float32)).astype(jnp.bfloat16).reshape(CAP, head_width)
        preact = jnp.dot(second_in, inner_weight, preferred_element_type=jnp.float32) + inner_bias
        active = jax.nn.gelu(preact, approximate=False).astype(jnp.bfloat16)
        group_ctx = context.reshape(CAP, N_TENSOR, head_width // N_TENSOR).astype(jnp.float32)
        group_dense = dense_weight.reshape(N_TENSOR, head_width // N_TENSOR, feature_width).astype(jnp.float32)
        group_act = active.reshape(CAP, N_TENSOR, FF // N_TENSOR).astype(jnp.float32)
        group_outer = outer_weight.reshape(N_TENSOR, FF // N_TENSOR, feature_width).astype(jnp.float32)
        partial_value = jnp.einsum('tgc,gcd->gtd', group_ctx, group_dense) + jnp.einsum('tgf,gfd->gtd', group_act, group_outer)
        rounded = lax.optimization_barrier(partial_value.astype(jnp.bfloat16))
        summed = lax.optimization_barrier(jnp.sum(rounded.astype(jnp.float32), axis=0))
        layer_out = (rank_rows.astype(jnp.float32) + summed + out_bias).astype(jnp.bfloat16)
        cot_float = rank_cot.astype(jnp.float32)
        outbias_grad = lax.optimization_barrier(jnp.sum(cot_float, axis=0))
        outer_grad = jnp.dot(active.T, rank_cot, preferred_element_type=jnp.float32)
        active_back = jnp.dot(rank_cot, outer_weight.T, preferred_element_type=jnp.float32)
        pre_grad = active_back * gelu_slope(preact)
        innerbias_grad = lax.optimization_barrier(jnp.sum(pre_grad, axis=0))
        pre_back = pre_grad.astype(jnp.bfloat16)
        inner_grad = jnp.dot(second_in.T, pre_back, preferred_element_type=jnp.float32)
        second_grad = jnp.dot(pre_back, inner_weight.T, preferred_element_type=jnp.float32)
        dense_grad = jnp.dot(context.T, rank_cot, preferred_element_type=jnp.float32)
        context_back = jnp.dot(rank_cot, dense_weight.T, preferred_element_type=jnp.float32).astype(jnp.bfloat16).reshape(CAP, HEADS, HD)
        weights_full = jnp.exp(scores - logsum)
        weights_bf = weights_full.astype(jnp.bfloat16)
        value_grad = jnp.einsum('hqk,qhd->khd', weights_bf.astype(jnp.float32), context_back.astype(jnp.float32))
        prob_grad = jnp.einsum('qhd,khd->hqk', context_back.astype(jnp.float32), values_bf.astype(jnp.float32))
        row_delta = lax.optimization_barrier(jnp.sum(weights_full * prob_grad, axis=-1, keepdims=True))
        score_back = (weights_full * (prob_grad - row_delta) * score_scale).astype(jnp.bfloat16)
        query_grad = jnp.einsum('hqk,khd->qhd', score_back.astype(jnp.float32), keys_bf.astype(jnp.float32))
        key_grad = jnp.einsum('hqk,qhd->khd', score_back.astype(jnp.float32), queries.astype(jnp.float32))
        qkv_back = jnp.stack([unrotate(query_grad, cosine, sine_table), unrotate(key_grad, cosine, sine_table), value_grad], axis=1)
        qkvbias_grad = lax.optimization_barrier(jnp.sum(qkv_back, axis=0)).reshape(3, head_width)
        qkv_backb = qkv_back.reshape(CAP, 3 * head_width).astype(jnp.bfloat16)
        qkv_grad = jnp.dot(first_in.T, qkv_backb, preferred_element_type=jnp.float32).reshape(feature_width, 3, head_width)
        first_grad = jnp.dot(qkv_backb, qkv_flat.T, preferred_element_type=jnp.float32)
        gain1_grad = lax.optimization_barrier(jnp.sum(first_grad * normed, axis=0))
        bias1_grad = lax.optimization_barrier(jnp.sum(first_grad, axis=0))
        gain2_grad = lax.optimization_barrier(jnp.sum(second_grad * normed, axis=0))
        bias2_grad = lax.optimization_barrier(jnp.sum(second_grad, axis=0))
        residual_grad = (cot_float + norm_back(first_grad, normed, inv_std, norm1_gain) + norm_back(second_grad, normed, inv_std, norm2_gain)).astype(jnp.bfloat16)
        terms = (gain1_grad, bias1_grad, gain2_grad, bias2_grad, qkv_grad, qkvbias_grad, dense_grad, inner_grad, innerbias_grad, outer_grad, outbias_grad)
        new_carry = tuple((held + term for held, term in zip(carry, terms)))
        return (new_carry, (layer_out, residual_grad))
    initial = (jnp.zeros((feature_width,), jnp.float32), jnp.zeros((feature_width,), jnp.float32), jnp.zeros((feature_width,), jnp.float32), jnp.zeros((feature_width,), jnp.float32), jnp.zeros((feature_width, 3, head_width), jnp.float32), jnp.zeros((3, head_width), jnp.float32), jnp.zeros((head_width, feature_width), jnp.float32), jnp.zeros((feature_width, FF), jnp.float32), jnp.zeros((FF,), jnp.float32), jnp.zeros((FF, feature_width), jnp.float32), jnp.zeros((feature_width,), jnp.float32))
    stacked = (residual.reshape(N_DP, CAP, feature_width), cotangent.reshape(N_DP, CAP, feature_width), seq_lengths)
    totals, (outputs, input_grads) = lax.scan(one_rank, initial, stacked)
    layer_out = outputs.reshape(N_DP * CAP, feature_width)
    residual_grad = input_grads.reshape(N_DP * CAP, feature_width)
    return (layer_out, residual_grad, totals[0], totals[1], totals[2], totals[3], totals[4], totals[5], totals[6], totals[7], totals[8], totals[9], totals[10])
```

```python
import functools
import math

import jax
import jax.numpy as jnp
from jax import lax
from jax.experimental import pallas as pl
from jax.experimental.pallas import tpu as pltpu
from jax.sharding import PartitionSpec as P

HD = 64
ROT = 16
MAXLEN = 512
EPSILON = 1e-05
MASKED_SCORE = -1e30
SQRT_HALF = 0.7071067811865476
INV_ROOT_TWO_PI = 0.3989422804014327
F32 = jnp.float32
BF16 = jnp.bfloat16
PAIR = 2 * HD
QROWS = 256
HIDDEN = 256
VMEM = 56 * 1024 * 1024


def dot(lhs, rhs, contract):
    return lax.dot_general(lhs, rhs, (contract, ((), ())), preferred_element_type=F32)


NN = ((1,), (0,))
NT = ((1,), (1,))
TN = ((0,), (0,))


def ffn_kernel(second_ref, cot_ref, inner_ref, bias_ref, outer_ref, active_ref, back_ref, grads_ref, biasgrad_ref):
    second = second_ref[...]
    cot = cot_ref[...]
    preact = dot(second, inner_ref[...], NN) + bias_ref[...]
    cdf = 0.5 * (1.0 + lax.erf(preact * SQRT_HALF))
    slope = cdf + preact * jnp.exp(-0.5 * preact * preact) * INV_ROOT_TWO_PI
    active = (preact * cdf).astype(BF16)
    active_ref[...] = active
    pre_grad = dot(cot, outer_ref[...], NT) * slope
    biasgrad_ref[...] = jnp.sum(pre_grad, axis=0, keepdims=True)
    back = pre_grad.astype(BF16)
    back_ref[...] = back
    grads_ref[0] = dot(second, back, TN).astype(BF16)
    outer = dot(active, cot, TN).astype(BF16)
    for c in range(outer.shape[1] // HIDDEN):
        grads_ref[1, c * HIDDEN : (c + 1) * HIDDEN, :] = outer[:, c * HIDDEN : (c + 1) * HIDDEN]


def ffn_slice(second_in, cot, inner_weight, inner_bias, outer_weight, first, count):
    rows, width = second_in.shape
    cols = count * HIDDEN
    whole = pl.BlockSpec((rows, width), lambda j: (0, 0))
    return pl.pallas_call(
        ffn_kernel,
        grid=(count,),
        in_specs=[
            whole,
            whole,
            pl.BlockSpec((width, HIDDEN), lambda j: (0, first + j)),
            pl.BlockSpec((1, HIDDEN), lambda j: (0, first + j)),
            pl.BlockSpec((HIDDEN, width), lambda j: (first + j, 0)),
        ],
        out_specs=[
            pl.BlockSpec((rows, HIDDEN), lambda j: (0, j)),
            pl.BlockSpec((rows, HIDDEN), lambda j: (0, j)),
            pl.BlockSpec((2, width, HIDDEN), lambda j: (0, 0, j)),
            pl.BlockSpec((1, HIDDEN), lambda j: (0, j)),
        ],
        out_shape=[
            jax.ShapeDtypeStruct((rows, cols), BF16),
            jax.ShapeDtypeStruct((rows, cols), BF16),
            jax.ShapeDtypeStruct((2, width, cols), BF16),
            jax.ShapeDtypeStruct((1, cols), F32),
        ],
        compiler_params=pltpu.CompilerParams(vmem_limit_bytes=VMEM),
        cost_estimate=pl.CostEstimate(
            flops=8 * rows * width * cols, bytes_accessed=20 * width * cols, transcendentals=2 * rows * cols
        ),
    )(second_in, cot, inner_weight, inner_bias, outer_weight)


def partner(values):
    half = ROT // 2
    lane = lax.broadcasted_iota(jnp.int32, values.shape, 1) % HD
    lanes = values.shape[1]
    return jnp.where(lane < half, pltpu.roll(values, lanes - half, 1), pltpu.roll(values, half, 1))


def attention_kernel(
    slots, first_ref, cot_ref, w_ref, wbias_ref, dense_ref, cos_ref, sin_ref, segq_ref, segk_ref,
    context_ref, back_ref, grads_ref, biasgrad_ref, mask_ref, dk_ref, dv_ref,
):
    rows = first_ref.shape[0]
    blocks = rows // QROWS
    reach = -(-(MAXLEN - 1) // QROWS)

    @pl.when(pl.program_id(0) == 0)
    def _():
        for i in range(blocks):
            low = max(0, i - reach) * QROWS
            span = (i + 1) * QROWS - low
            seg_q = segq_ref[i * QROWS : (i + 1) * QROWS, :]
            seg_k = segk_ref[:, low : low + span]
            q_at = lax.broadcasted_iota(jnp.int32, (QROWS, span), 0) + i * QROWS
            k_at = lax.broadcasted_iota(jnp.int32, (QROWS, span), 1) + low
            allowed = ((seg_q == seg_k) & (k_at <= q_at) & (seg_q < slots)) | (k_at == q_at)
            mask_ref[i * QROWS : (i + 1) * QROWS, :span] = jnp.where(allowed, 0.0, MASKED_SCORE)

    first = first_ref[...]
    cot = cot_ref[...]
    weight = jnp.concatenate([w_ref[0], w_ref[1], w_ref[2]], axis=1)
    bias = jnp.concatenate([wbias_ref[0], wbias_ref[1], wbias_ref[2]], axis=1)
    projected = dot(first, weight, NN) + bias
    cosine = cos_ref[...]
    sine = sin_ref[...]
    q = projected[:, :PAIR]
    k = projected[:, PAIR : 2 * PAIR]
    queries = (q * cosine + partner(q) * sine).astype(BF16)
    keys = (k * cosine + partner(k) * sine).astype(BF16)
    values = projected[:, 2 * PAIR :].astype(BF16)
    context_back = dot(cot, dense_ref[...], NT).astype(BF16)

    lane_head = lax.broadcasted_iota(jnp.int32, (QROWS, PAIR), 1) // HD
    scale = HD**-0.5
    dk_ref[...] = jnp.zeros_like(dk_ref)
    dv_ref[...] = jnp.zeros_like(dv_ref)
    contexts = []
    dqs = []
    for i in range(blocks):
        low = max(0, i - reach) * QROWS
        high = (i + 1) * QROWS
        mask = mask_ref[i * QROWS : high, : high - low]
        q_block = queries[i * QROWS : high]
        b_block = context_back[i * QROWS : high]
        k_block = keys[low:high]
        v_block = values[low:high]
        ctx = None
        for h in range(2):
            mine = lane_head == h
            q_head = jnp.where(mine, q_block, jnp.zeros_like(q_block))
            b_head = jnp.where(mine, b_block, jnp.zeros_like(b_block))
            scores = dot(q_head, k_block, NT) * scale + mask
            highest = jnp.max(scores, axis=1, keepdims=True)
            exponent = jnp.exp(scores - highest)
            total = jnp.sum(exponent, axis=1, keepdims=True)
            weights = exponent * (1.0 / total)
            weights_bf = weights.astype(BF16)
            prob_grad = dot(b_head, v_block, NT)
            delta = jnp.sum(weights * prob_grad, axis=1, keepdims=True)
            score_back = (weights * (prob_grad - delta)).astype(BF16)
            ctx_head = dot(weights_bf, v_block, NN)
            dq_head = dot(score_back, k_block, NN)
            dk_ref[low:high, :] += dot(score_back, q_head, TN)
            dv_ref[low:high, :] += dot(weights_bf, b_head, TN)
            ctx = ctx_head if h == 0 else jnp.where(mine, ctx_head, ctx)
            dq = dq_head if h == 0 else jnp.where(mine, dq_head, dq)
        contexts.append(ctx.astype(BF16))
        dqs.append(dq)
    context = jnp.concatenate(contexts, axis=0)
    context_ref[...] = context
    dq = jnp.concatenate(dqs, axis=0) * scale
    dk = dk_ref[...] * scale
    dv = dv_ref[...]
    dq = dq * cosine - partner(dq) * sine
    dk = dk * cosine - partner(dk) * sine
    back = jnp.concatenate([dq, dk, dv], axis=1)
    biasgrad_ref[0] = jnp.sum(back, axis=0, keepdims=True)
    back = back.astype(BF16)
    back_ref[0] = back
    weight_grad = dot(first, back, TN).astype(BF16)
    grads_ref[0] = weight_grad[:, : 2 * PAIR]
    grads_ref[1, :, :PAIR] = weight_grad[:, 2 * PAIR :]
    dense_grad = dot(context, cot, TN).astype(BF16)
    for c in range(dense_grad.shape[1] // PAIR):
        grads_ref[1, c * PAIR : (c + 1) * PAIR, PAIR:] = dense_grad[:, c * PAIR : (c + 1) * PAIR]


def attention_slice(first_in, cot, qkv, qkv_bias, dense_weight, cosine, sine, segment, slots, first, count):
    rows, width = first_in.shape
    reach = -(-(MAXLEN - 1) // QROWS)
    span = min(rows, (reach + 1) * QROWS)
    whole = pl.BlockSpec((rows, width), lambda j: (0, 0))
    table = pl.BlockSpec((rows, PAIR), lambda j: (0, 0))
    return pl.pallas_call(
        functools.partial(attention_kernel, slots),
        grid=(count,),
        in_specs=[
            whole,
            whole,
            pl.BlockSpec((3, width, PAIR), lambda j: (0, 0, first + j)),
            pl.BlockSpec((3, 1, PAIR), lambda j: (0, 0, first + j)),
            pl.BlockSpec((PAIR, width), lambda j: (first + j, 0)),
            table,
            table,
            pl.BlockSpec((rows, 1), lambda j: (0, 0)),
            pl.BlockSpec((1, rows), lambda j: (0, 0)),
        ],
        out_specs=[
            pl.BlockSpec((rows, PAIR), lambda j: (0, j)),
            pl.BlockSpec((1, rows, 3 * PAIR), lambda j: (j, 0, 0)),
            pl.BlockSpec((2, width, 2 * PAIR), lambda j: (0, 0, j)),
            pl.BlockSpec((1, 1, 3 * PAIR), lambda j: (j, 0, 0)),
        ],
        out_shape=[
            jax.ShapeDtypeStruct((rows, count * PAIR), BF16),
            jax.ShapeDtypeStruct((count, rows, 3 * PAIR), BF16),
            jax.ShapeDtypeStruct((2, width, count * 2 * PAIR), BF16),
            jax.ShapeDtypeStruct((count, 1, 3 * PAIR), F32),
        ],
        scratch_shapes=[
            pltpu.VMEM((rows, span), F32),
            pltpu.VMEM((rows, PAIR), F32),
            pltpu.VMEM((rows, PAIR), F32),
        ],
        compiler_params=pltpu.CompilerParams(vmem_limit_bytes=VMEM),
        cost_estimate=pl.CostEstimate(
            flops=count * 30 * rows * width * PAIR,
            bytes_accessed=16 * width * count * PAIR,
            transcendentals=count * 2 * rows * span,
        ),
    )(first_in, cot, qkv, qkv_bias, dense_weight, cosine, sine, segment.reshape(rows, 1), segment.reshape(1, rows))


def rings(size):
    if size == 16:
        return [(4, 4), (2, 2), (1, 2)]
    lengths = []
    left = size
    while left > 1:
        length = next(f for f in (2, 4, 3, 5, 7, left) if left % f == 0 and (f != 2 or not lengths))
        lengths.insert(0, length)
        left //= length
    out = []
    stride = 1
    for length in reversed(lengths):
        out.insert(0, (stride, length))
        stride *= length
    while len(out) < 3:
        out.insert(0, (stride, 1))
    return [(out[0][0], math.prod(l for _, l in out[:-2]))] + out[-2:] if len(out) > 3 else out


def ring_pairs(size, stride, length):
    return [(i, i + ((i // stride + 1) % length - i // stride % length) * stride) for i in range(size)]


def piece(values, index, length):
    axis = values.ndim - 2
    rows = values.shape[axis] // length
    return lax.dynamic_slice_in_dim(values, index * rows, rows, axis)


def ring_reduce(values, size, ring):
    stride, length = ring
    if length == 1:
        return values
    at = lax.axis_index("dp") // stride % length
    pairs = ring_pairs(size, stride, length)
    held = piece(values, (at + length - 1) % length, length)
    for step in range(length - 1):
        came = lax.ppermute(held, "dp", pairs)
        own = piece(values, (at + 2 * length - 2 - step) % length, length)
        held = (came.astype(F32) + own.astype(F32)).astype(BF16)
    return held


def ring_gather(held, size, ring):
    stride, length = ring
    if length == 1:
        return held
    at = lax.axis_index("dp") // stride % length
    pairs = ring_pairs(size, stride, length)
    axis = held.ndim - 2
    parts = [held]
    for _ in range(length - 1):
        parts.append(lax.ppermute(parts[-1], "dp", pairs))
    ordered = []
    for slot in range(length):
        chosen = parts[0]
        for back in range(1, length):
            chosen = jnp.where((at + length - back) % length == slot, parts[back], chosen)
        ordered.append(chosen)
    return jnp.concatenate(ordered, axis=axis)


def reduce_over_dp(grads, size):
    slow, mid, fast = rings(size)
    left = ring_reduce(grads[0], size, fast)
    right = ring_reduce(grads[1], size, mid)
    left = ring_reduce(left, size, mid)
    right = ring_reduce(right, size, fast)
    both = jnp.stack([left, right])
    both = ring_gather(ring_reduce(both, size, slow), size, slow)
    left = ring_gather(both[0], size, mid)
    right = ring_gather(both[1], size, fast)
    left = ring_gather(left, size, fast)
    right = ring_gather(right, size, mid)
    return left, right


def butterfly(values, axis, size):
    if size & (size - 1):
        return lax.psum(values, axis)
    step = 1
    while step < size:
        values = values + lax.ppermute(values, axis, [(i, i ^ step) for i in range(size)])
        step *= 2
    return values


def normalize(values):
    mean_val = jnp.mean(values, axis=-1, keepdims=True)
    centred = values - mean_val
    inv_std = lax.rsqrt(jnp.mean(centred * centred, axis=-1, keepdims=True) + EPSILON)
    return (centred * inv_std, inv_std)


def layout(lengths, row_count):
    slot_count = lengths.shape[0]
    places = jnp.arange(row_count, dtype=jnp.int32)
    seq_ends = jnp.cumsum(lengths)
    seq_starts = seq_ends - lengths
    segment = jnp.sum((places[:, None] >= seq_ends[None, :]).astype(jnp.int32), axis=1)
    member = segment[:, None] == jnp.arange(slot_count, dtype=jnp.int32)[None, :]
    position = places - jnp.sum(jnp.where(member, seq_starts[None, :], 0), axis=1)
    return (segment, position)


def rotary_tables(position):
    half = ROT // 2
    lane = jnp.arange(PAIR, dtype=jnp.int32) % HD
    frequency = jnp.exp(-(2.0 * (lane % half).astype(F32) / ROT) * math.log(10000.0))
    angle = position.astype(F32)[:, None] * jnp.where(lane < ROT, frequency, 0.0)[None, :]
    sign = jnp.where(lane < half, -1.0, jnp.where(lane < ROT, 1.0, 0.0))
    return (jnp.cos(angle), jnp.sin(angle) * sign[None, :])


def gather_rows(values, size):
    if size != 2:
        return lax.all_gather(values, "tensor", axis=0, tiled=True)
    other = lax.ppermute(values, "tensor", [(0, 1), (1, 0)])
    here = lax.axis_index("tensor")
    return jnp.concatenate([jnp.where(here == 0, values, other), jnp.where(here == 0, other, values)], axis=0)


def scatter_sum(values, size):
    if size != 2:
        return lax.psum_scatter(values, "tensor", scatter_dimension=0, tiled=True).astype(F32)
    rows = values.shape[0] // 2
    here = lax.axis_index("tensor")
    away = lax.dynamic_slice_in_dim(values, (1 - here) * rows, rows, 0).astype(BF16)
    mine = lax.dynamic_slice_in_dim(values, here * rows, rows, 0)
    return lax.ppermute(away, "tensor", [(0, 1), (1, 0)]).astype(F32) + mine.astype(F32)


def local(
    dp_size,
    tensor_size,
    residual,
    norm1_gain,
    norm1_bias,
    norm2_gain,
    norm2_bias,
    qkv_weight,
    qkv_bias,
    dense_weight,
    inner_weight,
    inner_bias,
    outer_weight,
    out_bias,
    cotangent,
    seq_lengths,
):
    local_rows, width = residual.shape
    head_width = qkv_weight.shape[2]
    hidden = inner_weight.shape[1]
    slots = seq_lengths.shape[1]

    gathered = gather_rows(residual, tensor_size)
    cot = gather_rows(cotangent, tensor_size)
    rows = gathered.shape[0]
    segment, position = layout(seq_lengths[0], rows)
    cosine, sine = rotary_tables(position)
    qkv = jnp.transpose(qkv_weight, (1, 0, 2))
    normed, inv_std = normalize(gathered.astype(F32))
    first_in = (normed * norm1_gain + norm1_bias).astype(BF16)
    second_in = (normed * norm2_gain + norm2_bias).astype(BF16)

    steps = hidden // HIDDEN
    per = max(1, steps // 4)
    ffn = [
        ffn_slice(second_in, cot, inner_weight, inner_bias.reshape(1, -1), outer_weight, at, per)
        for at in range(0, steps, per)
    ]
    pairs = head_width // PAIR
    per_pair = max(1, pairs // 2)
    attn = [
        attention_slice(
            first_in, cot, qkv, qkv_bias.reshape(3, 1, -1), dense_weight, cosine, sine, segment, slots, at, per_pair
        )
        for at in range(0, pairs, per_pair)
    ]
    ffn_sums = [reduce_over_dp(f[2], dp_size) for f in ffn]
    attn_sums = [reduce_over_dp(a[2], dp_size) for a in attn]

    active = jnp.concatenate([f[0] for f in ffn], axis=1)
    pre_back = jnp.concatenate([f[1] for f in ffn], axis=1)
    context = jnp.concatenate([a[0] for a in attn], axis=1)
    qkv_back = jnp.concatenate([a[1] for a in attn], axis=0)
    branch = (dot(context, dense_weight, NN) + dot(active, outer_weight, NN)).astype(BF16)
    summed = scatter_sum(branch, tensor_size)
    layer_out = (residual.astype(F32) + summed + out_bias).astype(BF16)

    back3 = qkv_back.reshape(pairs, rows, 3, PAIR).transpose(1, 2, 0, 3).reshape(rows, 3 * head_width)
    weight3 = jnp.transpose(qkv, (0, 2, 1)).reshape(3 * head_width, width)
    first_grad = dot(back3, weight3, NN)
    second_grad = dot(pre_back, inner_weight, NT)
    combined = scatter_sum(first_grad * norm1_gain + second_grad * norm2_gain, tensor_size)
    own_normed, own_inv = normalize(residual.astype(F32))
    residual_grad = (
        cotangent.astype(F32)
        + own_inv
        * (
            combined
            - jnp.mean(combined, axis=-1, keepdims=True)
            - own_normed * jnp.mean(combined * own_normed, axis=-1, keepdims=True)
        )
    ).astype(BF16)

    over_all = jnp.stack(
        [
            jnp.sum(first_grad * normed, axis=0),
            jnp.sum(first_grad, axis=0),
            jnp.sum(second_grad * normed, axis=0),
            jnp.sum(second_grad, axis=0),
            jnp.sum(cotangent.astype(F32), axis=0),
        ]
    ).reshape(-1)
    over_all = butterfly(over_all, "tensor", tensor_size)
    qkvbias = jnp.concatenate([a[3] for a in attn], axis=0).reshape(pairs, 3, PAIR).transpose(1, 0, 2).reshape(-1)
    innerbias = jnp.concatenate([f[3] for f in ffn], axis=1).reshape(-1)
    vectors = butterfly(jnp.concatenate([over_all, qkvbias, innerbias]), "dp", dp_size)
    ends = [width * i for i in range(1, 6)] + [5 * width + 3 * head_width]
    gain1_grad, bias1_grad, gain2_grad, bias2_grad, outbias_grad, qkvbias_grad, innerbias_grad = jnp.split(vectors, ends)

    inner_grad = jnp.concatenate([s[0] for s in ffn_sums], axis=1).astype(F32)
    outer_grad = jnp.concatenate(
        [
            s[1].reshape(width // HIDDEN, HIDDEN, per, HIDDEN).transpose(2, 1, 0, 3).reshape(per * HIDDEN, width)
            for s in ffn_sums
        ],
        axis=0,
    ).astype(F32)
    qk_parts = [s[0].reshape(width, per_pair, 2, PAIR) for s in attn_sums]
    vd_parts = [s[1].reshape(width, per_pair, 2, PAIR) for s in attn_sums]
    qk_grad = jnp.concatenate(qk_parts, axis=1).transpose(0, 2, 1, 3).reshape(width, 2, head_width)
    v_grad = jnp.concatenate([p[:, :, 0] for p in vd_parts], axis=1).reshape(width, 1, head_width)
    qkv_grad = jnp.concatenate([qk_grad, v_grad], axis=1).astype(F32)
    dense_grad = jnp.concatenate(
        [
            p[:, :, 1].reshape(width // PAIR, PAIR, per_pair, PAIR).transpose(2, 1, 0, 3).reshape(per_pair * PAIR, width)
            for p in vd_parts
        ],
        axis=0,
    ).astype(F32)
    return (
        layer_out,
        residual_grad,
        gain1_grad,
        bias1_grad,
        gain2_grad,
        bias2_grad,
        qkv_grad,
        qkvbias_grad.reshape(3, head_width),
        dense_grad,
        inner_grad,
        innerbias_grad,
        outer_grad,
        outbias_grad,
    )


def solution(mesh):
    rows = P(("dp", "tensor"), None)
    return jax.shard_map(
        functools.partial(local, mesh.shape["dp"], mesh.shape["tensor"]),
        mesh=mesh,
        in_specs=(
            rows,
            P(),
            P(),
            P(),
            P(),
            P(None, None, "tensor"),
            P(None, "tensor"),
            P("tensor", None),
            P(None, "tensor"),
            P("tensor"),
            P("tensor", None),
            P(),
            rows,
            P("dp", None),
        ),
        out_specs=(
            rows,
            rows,
            P(),
            P(),
            P(),
            P(),
            P(None, None, "tensor"),
            P(None, "tensor"),
            P("tensor", None),
            P(None, "tensor"),
            P("tensor"),
            P("tensor", None),
            P(),
        ),
        check_vma=False,
    )
```

```python
import functools
import math

import jax
import jax.numpy as jnp
from jax import lax
from jax.experimental import pallas as pl
from jax.experimental.pallas import tpu as pltpu
from jax.sharding import PartitionSpec as P

HD = 64
ROT = 16
MAXLEN = 512
EPSILON = 1e-05
MASKED_SCORE = -1e30
SQRT_HALF = 0.7071067811865476
INV_ROOT_TWO_PI = 0.3989422804014327
F32 = jnp.float32
BF16 = jnp.bfloat16
PAIR = 2 * HD
QROWS = 256
HIDDEN = 256
VMEM = 56 * 1024 * 1024


def dot(lhs, rhs, contract):
    return lax.dot_general(lhs, rhs, (contract, ((), ())), preferred_element_type=F32)


NN = ((1,), (0,))
NT = ((1,), (1,))
TN = ((0,), (0,))


ANY = pl.BlockSpec(memory_space=pl.ANY)
PARAMS = pltpu.CompilerParams(vmem_limit_bytes=VMEM)


def after(kernel, inputs, held):
    def body(*refs):
        kernel(*refs[:inputs], *refs[inputs + held :])

    return body


def prep_kernel(slot_ref, own_ref, other_ref, own_cot_ref, other_cot_ref, g1_ref, b1_ref, g2_ref, b2_ref,
                normed_ref, first_ref, second_ref, cot_ref):
    def emit(x_ref, c_ref):
        x = x_ref[...].astype(F32)
        centred = x - jnp.mean(x, axis=1, keepdims=True)
        normed = centred * lax.rsqrt(jnp.mean(centred * centred, axis=1, keepdims=True) + EPSILON)
        normed_ref[...] = normed
        first_ref[...] = (normed * g1_ref[...] + b1_ref[...]).astype(BF16)
        second_ref[...] = (normed * g2_ref[...] + b2_ref[...]).astype(BF16)
        cot_ref[...] = c_ref[...]

    pl.when(pl.program_id(0) == 0)(lambda: emit(own_ref, own_cot_ref))
    pl.when(pl.program_id(0) == 1)(lambda: emit(other_ref, other_cot_ref))


def prep(own, other, own_cot, other_cot, here, gains):
    rows, width = own.shape
    block = min(rows, 256)
    count = rows // block
    mine = pl.BlockSpec((block, width), lambda j, i, slot: (jnp.where(j == 0, i, count - 1), 0))
    theirs = pl.BlockSpec((block, width), lambda j, i, slot: (jnp.where(j == 0, 0, i), 0))
    vector = pl.BlockSpec((1, width), lambda j, i, slot: (0, 0))
    out = pl.BlockSpec((block, width), lambda j, i, slot: (slot[j] * count + i, 0))
    return pl.pallas_call(
        prep_kernel,
        grid_spec=pltpu.PrefetchScalarGridSpec(
            num_scalar_prefetch=1,
            grid=(2, count),
            in_specs=[mine, theirs, mine, theirs] + [vector] * 4,
            out_specs=[out] * 4,
        ),
        out_shape=[
            jax.ShapeDtypeStruct((2 * rows, width), F32),
            jax.ShapeDtypeStruct((2 * rows, width), BF16),
            jax.ShapeDtypeStruct((2 * rows, width), BF16),
            jax.ShapeDtypeStruct((2 * rows, width), BF16),
        ],
        compiler_params=PARAMS,
        cost_estimate=pl.CostEstimate(flops=rows * width * 40, bytes_accessed=rows * width * 28, transcendentals=0),
    )(jnp.stack([here, 1 - here]), own, other, own_cot, other_cot, *[g.reshape(1, -1) for g in gains])


def ffn_kernel(second_ref, cot_ref, inner_ref, bias_ref, outer_ref, active_ref, back_ref, left_ref, right_ref, biasgrad_ref):
    second = second_ref[...]
    cot = cot_ref[...]
    preact = dot(second, inner_ref[...], NN) + bias_ref[...]
    cdf = 0.5 * (1.0 + lax.erf(preact * SQRT_HALF))
    slope = cdf + preact * jnp.exp(-0.5 * preact * preact) * INV_ROOT_TWO_PI
    active = (preact * cdf).astype(BF16)
    active_ref[...] = active
    pre_grad = dot(cot, outer_ref[...], NT) * slope
    biasgrad_ref[...] = jnp.sum(pre_grad, axis=0, keepdims=True)
    back = pre_grad.astype(BF16)
    back_ref[...] = back
    left_ref[...] = dot(second, back, TN).astype(BF16)
    outer = dot(active, cot, TN).astype(BF16)
    cols = right_ref.shape[2]
    for c in range(right_ref.shape[0]):
        right_ref[c] = outer[:, c * cols : (c + 1) * cols]


def ffn_slice(second_in, cot, inner_weight, inner_bias, outer_weight, first, count, held=()):
    rows, width = second_in.shape
    cols = count * HIDDEN
    whole = pl.BlockSpec((rows, width), lambda j: (0, 0))
    return pl.pallas_call(
        after(ffn_kernel, 5, len(held)),
        grid=(count,),
        in_specs=[
            whole,
            whole,
            pl.BlockSpec((width, HIDDEN), lambda j: (0, first + j)),
            pl.BlockSpec((1, HIDDEN), lambda j: (0, first + j)),
            pl.BlockSpec((HIDDEN, width), lambda j: (first + j, 0)),
        ]
        + [ANY] * len(held),
        out_specs=[
            pl.BlockSpec((rows, HIDDEN), lambda j: (0, j)),
            pl.BlockSpec((rows, HIDDEN), lambda j: (0, j)),
            pl.BlockSpec((width, HIDDEN), lambda j: (0, j)),
            pl.BlockSpec((width // cols, HIDDEN, cols), lambda j: (0, j, 0)),
            pl.BlockSpec((1, HIDDEN), lambda j: (0, j)),
        ],
        out_shape=[
            jax.ShapeDtypeStruct((rows, cols), BF16),
            jax.ShapeDtypeStruct((rows, cols), BF16),
            jax.ShapeDtypeStruct((width, cols), BF16),
            jax.ShapeDtypeStruct((width // cols, cols, cols), BF16),
            jax.ShapeDtypeStruct((1, cols), F32),
        ],
        compiler_params=PARAMS,
        cost_estimate=pl.CostEstimate(
            flops=8 * rows * width * cols, bytes_accessed=20 * width * cols, transcendentals=2 * rows * cols
        ),
    )(second_in, cot, inner_weight, inner_bias, outer_weight, *held)


def partner(values):
    half = ROT // 2
    lane = lax.broadcasted_iota(jnp.int32, values.shape, 1) % HD
    lanes = values.shape[1]
    return jnp.where(lane < half, pltpu.roll(values, lanes - half, 1), pltpu.roll(values, half, 1))


def attention_kernel(
    slots, first_ref, cot_ref, w_ref, wbias_ref, dense_ref, cos_ref, sin_ref, segq_ref, segk_ref,
    context_ref, back_ref, grads_ref, dense_grads_ref, biasgrad_ref, mask_ref, dk_ref, dv_ref,
):
    rows = first_ref.shape[0]
    blocks = rows // QROWS
    reach = -(-(MAXLEN - 1) // QROWS)

    @pl.when(pl.program_id(0) == 0)
    def _():
        for i in range(blocks):
            low = max(0, i - reach) * QROWS
            span = (i + 1) * QROWS - low
            seg_q = segq_ref[i * QROWS : (i + 1) * QROWS, :]
            seg_k = segk_ref[:, low : low + span]
            q_at = lax.broadcasted_iota(jnp.int32, (QROWS, span), 0) + i * QROWS
            k_at = lax.broadcasted_iota(jnp.int32, (QROWS, span), 1) + low
            allowed = ((seg_q == seg_k) & (k_at <= q_at) & (seg_q < slots)) | (k_at == q_at)
            mask_ref[i * QROWS : (i + 1) * QROWS, :span] = jnp.where(allowed, 0.0, MASKED_SCORE)

    first = first_ref[...]
    cot = cot_ref[...]
    weight = jnp.concatenate([w_ref[0], w_ref[1], w_ref[2]], axis=1)
    bias = jnp.concatenate([wbias_ref[0], wbias_ref[1], wbias_ref[2]], axis=1)
    projected = dot(first, weight, NN) + bias
    cosine = cos_ref[...]
    sine = sin_ref[...]
    q = projected[:, :PAIR]
    k = projected[:, PAIR : 2 * PAIR]
    queries = (q * cosine + partner(q) * sine).astype(BF16)
    keys = (k * cosine + partner(k) * sine).astype(BF16)
    values = projected[:, 2 * PAIR :].astype(BF16)
    context_back = dot(cot, dense_ref[...], NT).astype(BF16)

    lane_head = lax.broadcasted_iota(jnp.int32, (QROWS, PAIR), 1) // HD
    scale = HD**-0.5
    dk_ref[...] = jnp.zeros_like(dk_ref)
    dv_ref[...] = jnp.zeros_like(dv_ref)
    contexts = []
    dqs = []
    for i in range(blocks):
        low = max(0, i - reach) * QROWS
        high = (i + 1) * QROWS
        mask = mask_ref[i * QROWS : high, : high - low]
        q_block = queries[i * QROWS : high]
        b_block = context_back[i * QROWS : high]
        k_block = keys[low:high]
        v_block = values[low:high]
        ctx = None
        for h in range(2):
            mine = lane_head == h
            q_head = jnp.where(mine, q_block, jnp.zeros_like(q_block))
            b_head = jnp.where(mine, b_block, jnp.zeros_like(b_block))
            scores = dot(q_head, k_block, NT) * scale + mask
            highest = jnp.max(scores, axis=1, keepdims=True)
            exponent = jnp.exp(scores - highest)
            total = jnp.sum(exponent, axis=1, keepdims=True)
            weights = exponent * (1.0 / total)
            weights_bf = weights.astype(BF16)
            prob_grad = dot(b_head, v_block, NT)
            delta = jnp.sum(weights * prob_grad, axis=1, keepdims=True)
            score_back = (weights * (prob_grad - delta)).astype(BF16)
            ctx_head = dot(weights_bf, v_block, NN)
            dq_head = dot(score_back, k_block, NN)
            dk_ref[low:high, :] += dot(score_back, q_head, TN)
            dv_ref[low:high, :] += dot(weights_bf, b_head, TN)
            ctx = ctx_head if h == 0 else jnp.where(mine, ctx_head, ctx)
            dq = dq_head if h == 0 else jnp.where(mine, dq_head, dq)
        contexts.append(ctx.astype(BF16))
        dqs.append(dq)
    context = jnp.concatenate(contexts, axis=0)
    context_ref[...] = context
    dq = jnp.concatenate(dqs, axis=0) * scale
    dk = dk_ref[...] * scale
    dv = dv_ref[...]
    dq = dq * cosine - partner(dq) * sine
    dk = dk * cosine - partner(dk) * sine
    back = jnp.concatenate([dq, dk, dv], axis=1)
    biasgrad_ref[...] = jnp.sum(back, axis=0, keepdims=True)
    back = back.astype(BF16)
    back_ref[...] = back
    weight_grad = dot(first, back, TN).astype(BF16)
    for c in range(3):
        grads_ref[c] = weight_grad[:, c * PAIR : (c + 1) * PAIR]
    dense_grads_ref[...] = dot(context, cot, TN).astype(BF16)


def attention_pair(first_in, cot, qkv, qkv_bias, dense_weight, cosine, sine, segment, slots, at, held=()):
    rows, width = first_in.shape
    reach = -(-(MAXLEN - 1) // QROWS)
    span = min(rows, (reach + 1) * QROWS)
    whole = pl.BlockSpec((rows, width), lambda j: (0, 0))
    table = pl.BlockSpec((rows, PAIR), lambda j: (0, 0))
    return pl.pallas_call(
        after(functools.partial(attention_kernel, slots), 9, len(held)),
        grid=(1,),
        in_specs=[
            whole,
            whole,
            pl.BlockSpec((3, width, PAIR), lambda j: (0, 0, at)),
            pl.BlockSpec((3, 1, PAIR), lambda j: (0, 0, at)),
            pl.BlockSpec((PAIR, width), lambda j: (at, 0)),
            table,
            table,
            pl.BlockSpec((rows, 1), lambda j: (0, 0)),
            pl.BlockSpec((1, rows), lambda j: (0, 0)),
        ]
        + [ANY] * len(held),
        out_specs=[
            pl.BlockSpec((rows, PAIR), lambda j: (0, 0)),
            pl.BlockSpec((rows, 3 * PAIR), lambda j: (0, 0)),
            pl.BlockSpec((3, width, PAIR), lambda j: (0, 0, 0)),
            pl.BlockSpec((PAIR, width), lambda j: (0, 0)),
            pl.BlockSpec((1, 3 * PAIR), lambda j: (0, 0)),
        ],
        out_shape=[
            jax.ShapeDtypeStruct((rows, PAIR), BF16),
            jax.ShapeDtypeStruct((rows, 3 * PAIR), BF16),
            jax.ShapeDtypeStruct((3, width, PAIR), BF16),
            jax.ShapeDtypeStruct((PAIR, width), BF16),
            jax.ShapeDtypeStruct((1, 3 * PAIR), F32),
        ],
        scratch_shapes=[
            pltpu.VMEM((rows, span), F32),
            pltpu.VMEM((rows, PAIR), F32),
            pltpu.VMEM((rows, PAIR), F32),
        ],
        compiler_params=PARAMS,
        cost_estimate=pl.CostEstimate(
            flops=30 * rows * width * PAIR,
            bytes_accessed=16 * width * PAIR,
            transcendentals=2 * rows * span,
        ),
    )(first_in, cot, qkv, qkv_bias, dense_weight, cosine, sine, segment.reshape(rows, 1), segment.reshape(1, rows), *held)


def branch_kernel(contexts, actives, slot_ref, *refs):
    context = jnp.concatenate([r[...] for r in refs[:contexts]], axis=1)
    active = jnp.concatenate([r[...] for r in refs[contexts : contexts + actives]], axis=1)
    dense_ref, outer_ref, away_ref, own_ref = refs[contexts + actives :]
    branch = (dot(context, dense_ref[...], NN) + dot(active, outer_ref[...], NN)).astype(BF16)

    @pl.when(pl.program_id(0) == 0)
    def _():
        away_ref[...] = branch

    @pl.when(pl.program_id(0) == 1)
    def _():
        own_ref[...] = branch


def back_kernel(qkv_backs, pre_backs, slot_ref, *refs):
    lanes = refs[:qkv_backs]
    pre_back = jnp.concatenate([r[...] for r in refs[qkv_backs : qkv_backs + pre_backs]], axis=1)
    qkv_ref, inner_ref, g1_ref, g2_ref, normed_ref, away_ref, own_ref, sums_ref = refs[qkv_backs + pre_backs :]
    first = None
    for c in range(3):
        part = jnp.concatenate([r[:, c * PAIR : (c + 1) * PAIR] for r in lanes], axis=1)
        term = dot(part, qkv_ref[c], NT)
        first = term if first is None else first + term
    second = dot(pre_back, inner_ref[...], NT)
    combined = first * g1_ref[...] + second * g2_ref[...]
    normed = normed_ref[...]
    sums = jnp.concatenate(
        [jnp.sum(v, axis=0, keepdims=True) for v in (first * normed, first, second * normed, second)], axis=0
    )

    @pl.when((pl.program_id(0) == 0) & (pl.program_id(1) == 0))
    def _():
        sums_ref[...] = jnp.zeros_like(sums_ref)

    sums_ref[...] += sums

    @pl.when(pl.program_id(0) == 0)
    def _():
        away_ref[...] = combined.astype(BF16)

    @pl.when(pl.program_id(0) == 1)
    def _():
        own_ref[...] = combined


def rows_call(kernel, here, sliced, whole, by_rows, own_type, sums, held, flops):
    rows = sliced[0].shape[0]
    width = whole[0].shape[-1] if whole[0].ndim == 2 else whole[0].shape[1]
    half = rows // 2
    block = min(half, 256)
    count = half // block
    at = lambda j, i, slot: (slot[j] * count + i, 0)
    in_specs = [pl.BlockSpec((block, v.shape[1]), at) for v in sliced]
    in_specs += [pl.BlockSpec(v.shape, lambda j, i, slot, n=v.ndim: (0,) * n) for v in whole]
    in_specs += [pl.BlockSpec((block, v.shape[1]), at) for v in by_rows]
    out_specs = [
        pl.BlockSpec((block, width), lambda j, i, slot: (jnp.where(j == 0, i, count - 1), 0)),
        pl.BlockSpec((block, width), lambda j, i, slot: (jnp.where(j == 0, 0, i), 0)),
    ]
    out_shape = [jax.ShapeDtypeStruct((half, width), BF16), jax.ShapeDtypeStruct((half, width), own_type)]
    if sums:
        out_specs.append(pl.BlockSpec((sums, width), lambda j, i, slot: (0, 0)))
        out_shape.append(jax.ShapeDtypeStruct((sums, width), F32))
    return pl.pallas_call(
        after(kernel, 1 + len(in_specs), len(held)),
        grid_spec=pltpu.PrefetchScalarGridSpec(
            num_scalar_prefetch=1, grid=(2, count), in_specs=in_specs + [ANY] * len(held), out_specs=out_specs
        ),
        out_shape=out_shape,
        compiler_params=PARAMS,
        cost_estimate=pl.CostEstimate(flops=flops, bytes_accessed=16 * rows * width, transcendentals=0),
    )(jnp.stack([1 - here, here]), *sliced, *whole, *by_rows, *held)


def rings(size):
    fast = 2 if size % 2 == 0 else 1
    mid = 4 if size % 32 == 0 else 2 if size % 4 == 0 else 1
    return [(fast * mid, size // (fast * mid)), (fast, mid), (1, fast)]


def position(ring):
    return lax.axis_index("dp") // ring[0] % ring[1]


def hop(values, size, ring):
    stride, length = ring
    pairs = [(i, i + ((i // stride + 1) % length - i // stride % length) * stride) for i in range(size)]
    return lax.ppermute(values, "dp", pairs)


def rows_of(values, index, length):
    rows = values.shape[0] // length
    return lax.dynamic_slice_in_dim(values, index * rows, rows, 0)


def add(came, own):
    return (came.astype(F32) + own.astype(F32)).astype(BF16)


def ring_reduce(values, size, ring):
    length = ring[1]
    if length == 1:
        return values
    at = position(ring)
    held = rows_of(values, (at + length - 1) % length, length)
    for step in range(length - 1):
        yield [held]
        came = hop(held, size, ring)
        held = add(came, rows_of(values, (at + 2 * length - 2 - step) % length, length))
    return held


def ring_pieces(held, size, ring):
    pieces = [held]
    for _ in range(ring[1] - 1):
        yield [pieces[-1]]
        pieces.append(hop(pieces[-1], size, ring))
    return pieces


def slots_of(ring):
    at = position(ring)
    return [(at + ring[1] - back) % ring[1] for back in range(ring[1])]


def join(pieces, ring):
    slots = slots_of(ring)
    ordered = []
    for slot in range(ring[1]):
        chosen = pieces[0]
        for back in range(1, ring[1]):
            chosen = jnp.where(slots[back] == slot, pieces[back], chosen)
        ordered.append(chosen)
    return jnp.concatenate(ordered, axis=0)


def together(one, two):
    results = [None, None]
    live = [one, two]
    while any(g is not None for g in live):
        held = []
        for k, g in enumerate(live):
            if g is None:
                continue
            try:
                held += next(g)
            except StopIteration as stop:
                results[k] = stop.value
                live[k] = None
        if held:
            yield held
    return results


def reduce_over_dp(left, right, size):
    slow, mid, fast = rings(size)
    left, right = yield from together(ring_reduce(left, size, fast), ring_reduce(right, size, mid))
    left, right = yield from together(ring_reduce(left, size, mid), ring_reduce(right, size, fast))
    both = jnp.stack([left, right])
    step = 1
    while step < slow[1]:
        yield [both]
        both = add(lax.ppermute(both, "dp", [(i, i ^ (step * slow[0])) for i in range(size)]), both)
        step *= 2
    left, right = yield from together(ring_pieces(both[0], size, mid), ring_pieces(both[1], size, fast))
    left, right = join(left, mid), join(right, fast)
    return (yield from together(ring_pieces(left, size, fast), ring_pieces(right, size, mid)))


def place_kernel(count, tile, slot_ref, *refs):
    out_ref = refs[-1]
    for k in range(count):

        @pl.when(pl.program_id(0) == k)
        def _():
            if tile:
                for t in range(refs[k].shape[0] // tile):
                    out_ref[:, t * tile : (t + 1) * tile] = refs[k][t * tile : (t + 1) * tile, :].astype(F32)
            else:
                out_ref[...] = refs[k][...].astype(F32)


def place(total, shape, pieces, ring, at, across):
    count = len(pieces)
    rows, cols = pieces[0].shape
    if across:
        out_spec = pl.BlockSpec((cols, rows), lambda j, slot: (at, slot[j]))
    else:
        out_spec = pl.BlockSpec((rows, cols), lambda j, slot: (slot[j], at))
    kernel = functools.partial(place_kernel, count, cols if across else 0)
    extra = [] if total is None else [total]
    return pl.pallas_call(
        after(kernel, 1 + count, len(extra)),
        grid_spec=pltpu.PrefetchScalarGridSpec(
            num_scalar_prefetch=1,
            grid=(count,),
            in_specs=[pl.BlockSpec((rows, cols), lambda j, slot: (0, 0))] * count + [ANY] * len(extra),
            out_specs=out_spec,
        ),
        out_shape=jax.ShapeDtypeStruct(shape, F32),
        input_output_aliases={1 + count: 0} if extra else {},
        compiler_params=PARAMS,
        cost_estimate=pl.CostEstimate(flops=0, bytes_accessed=6 * count * rows * cols, transcendentals=0),
    )(jnp.stack(slots_of(ring)), *pieces, *extra)


def butterfly(values, axis, size):
    if size & (size - 1):
        return lax.psum(values, axis)
    step = 1
    while step < size:
        values = values + lax.ppermute(values, axis, [(i, i ^ step) for i in range(size)])
        step *= 2
    return values


class Rounds:
    def __init__(self):
        self.live = []
        self.done = {}

    def add(self, name, steps):
        self.live.append((name, steps))

    def turn(self):
        held = []
        left = []
        for name, steps in self.live:
            try:
                held += next(steps)
                left.append((name, steps))
            except StopIteration as stop:
                self.done[name] = stop.value
        self.live = left
        return held


def normalize(values):
    mean_val = jnp.mean(values, axis=-1, keepdims=True)
    centred = values - mean_val
    inv_std = lax.rsqrt(jnp.mean(centred * centred, axis=-1, keepdims=True) + EPSILON)
    return (centred * inv_std, inv_std)


def layout(lengths, row_count):
    slot_count = lengths.shape[0]
    places = jnp.arange(row_count, dtype=jnp.int32)
    seq_ends = jnp.cumsum(lengths)
    seq_starts = seq_ends - lengths
    segment = jnp.sum((places[:, None] >= seq_ends[None, :]).astype(jnp.int32), axis=1)
    member = segment[:, None] == jnp.arange(slot_count, dtype=jnp.int32)[None, :]
    place = places - jnp.sum(jnp.where(member, seq_starts[None, :], 0), axis=1)
    return (segment, place)


def rotary_tables(places):
    half = ROT // 2
    lane = jnp.arange(PAIR, dtype=jnp.int32) % HD
    frequency = jnp.exp(-(2.0 * (lane % half).astype(F32) / ROT) * math.log(10000.0))
    angle = places.astype(F32)[:, None] * jnp.where(lane < ROT, frequency, 0.0)[None, :]
    sign = jnp.where(lane < half, -1.0, jnp.where(lane < ROT, 1.0, 0.0))
    return (jnp.cos(angle), jnp.sin(angle) * sign[None, :])


def local(
    dp_size,
    tensor_size,
    residual,
    norm1_gain,
    norm1_bias,
    norm2_gain,
    norm2_bias,
    qkv_weight,
    qkv_bias,
    dense_weight,
    inner_weight,
    inner_bias,
    outer_weight,
    out_bias,
    cotangent,
    seq_lengths,
):
    width = residual.shape[1]
    head_width = qkv_weight.shape[2]
    hidden = inner_weight.shape[1]
    slots = seq_lengths.shape[1]
    here = lax.axis_index("tensor")
    swap = [(0, 1), (1, 0)]

    if tensor_size == 2:
        other = lax.ppermute(residual, "tensor", swap)
        other_cot = lax.ppermute(cotangent, "tensor", swap)
        parts = (residual, other, cotangent, other_cot)
        order = here
    else:
        gathered = lax.all_gather(residual, "tensor", axis=0, tiled=True)
        gathered_cot = lax.all_gather(cotangent, "tensor", axis=0, tiled=True)
        middle = gathered.shape[0] // 2
        parts = (gathered[:middle], gathered[middle:], gathered_cot[:middle], gathered_cot[middle:])
        order = jnp.int32(0)
    normed, first_in, second_in, cot = prep(*parts, order, (norm1_gain, norm1_bias, norm2_gain, norm2_bias))
    rows = cot.shape[0]

    rounds = Rounds()
    ffn = []
    steps = hidden // HIDDEN
    per = max(1, steps // 4)

    def feed_forward():
        at = len(ffn) * per
        held = rounds.turn()
        out = ffn_slice(second_in, cot, inner_weight, inner_bias.reshape(1, -1), outer_weight, at, per, held)
        rounds.add(len(ffn), reduce_over_dp(out[2], out[3].reshape(width, per * HIDDEN), dp_size))
        ffn.append(out)

    early = (steps // per + 1) // 2
    for _ in range(early):
        feed_forward()

    lengths, late_qkv, _ = lax.optimization_barrier((seq_lengths, qkv_weight, ffn[0][4]))
    segment, places = layout(lengths[0], rows)
    cosine, sine = rotary_tables(places)
    qkv = jnp.transpose(late_qkv, (1, 0, 2))
    attn = []
    for pair in range(head_width // PAIR):
        held = rounds.turn()
        attn.append(
            attention_pair(
                first_in, cot, qkv, qkv_bias.reshape(3, 1, -1), dense_weight, cosine, sine, segment, slots, pair, held
            )
        )
    attn_sums = lax.psum(([a[2] for a in attn], [a[3] for a in attn]), "dp")
    while len(ffn) * per < steps:
        feed_forward()

    order = here if tensor_size == 2 else jnp.int32(1)
    held = rounds.turn()
    branch_away, branch_own = rows_call(
        functools.partial(branch_kernel, len(attn), len(ffn)), order, [a[0] for a in attn] + [f[0] for f in ffn],
        [dense_weight, outer_weight], [], BF16, 0, held, 2 * rows * width * (head_width + hidden),
    )
    held = rounds.turn()
    away, own, sums = rows_call(
        functools.partial(back_kernel, len(attn), len(ffn)), order, [a[1] for a in attn] + [f[1] for f in ffn],
        [qkv, inner_weight, norm1_gain.reshape(1, -1), norm2_gain.reshape(1, -1)], [normed], F32, 4, held,
        2 * rows * width * (3 * head_width + hidden),
    )
    if tensor_size == 2:
        summed = lax.ppermute(branch_away, "tensor", swap).astype(F32) + branch_own.astype(F32)
        combined = lax.ppermute(away, "tensor", swap).astype(F32) + own
    else:
        scatter = functools.partial(lax.psum_scatter, axis_name="tensor", scatter_dimension=0, tiled=True)
        summed = scatter(jnp.concatenate([branch_away, branch_own], axis=0)).astype(F32)
        combined = scatter(jnp.concatenate([away.astype(F32), own], axis=0))
    layer_out = (residual.astype(F32) + summed + out_bias).astype(BF16)
    own_normed, own_inv = normalize(residual.astype(F32))
    residual_grad = (
        cotangent.astype(F32)
        + own_inv
        * (
            combined
            - jnp.mean(combined, axis=-1, keepdims=True)
            - own_normed * jnp.mean(combined * own_normed, axis=-1, keepdims=True)
        )
    ).astype(BF16)

    over_all = jnp.concatenate([sums, jnp.sum(cotangent.astype(F32), axis=0, keepdims=True)], axis=0).reshape(-1)
    over_all = butterfly(over_all, "tensor", tensor_size)
    qkvbias = jnp.concatenate([a[4].reshape(3, PAIR) for a in attn], axis=1).reshape(-1)
    innerbias = jnp.concatenate([f[4] for f in ffn], axis=1).reshape(-1)
    vectors = butterfly(jnp.concatenate([over_all, qkvbias, innerbias]), "dp", dp_size)
    ends = [width * i for i in range(1, 6)] + [5 * width + 3 * head_width]
    gain1_grad, bias1_grad, gain2_grad, bias2_grad, outbias_grad, qkvbias_grad, innerbias_grad = jnp.split(vectors, ends)

    while rounds.live:
        rounds.turn()
    _, mid, fast = rings(dp_size)
    inner_grad = None
    outer_grad = None
    for k in range(len(ffn)):
        left, right = rounds.done[k]
        inner_grad = place(inner_grad, (width, hidden), left, fast, k, False)
        outer_grad = place(outer_grad, (hidden, width), right, mid, k, True)
    qkv_sums, dense_sums = attn_sums
    qkv_grad = jnp.concatenate([g.transpose(1, 0, 2) for g in qkv_sums], axis=2).astype(F32)
    dense_grad = jnp.concatenate(dense_sums, axis=0).astype(F32)
    return (
        layer_out,
        residual_grad,
        gain1_grad,
        bias1_grad,
        gain2_grad,
        bias2_grad,
        qkv_grad,
        qkvbias_grad.reshape(3, head_width),
        dense_grad,
        inner_grad,
        innerbias_grad,
        outer_grad,
        outbias_grad,
    )


def solution(mesh):
    rows = P(("dp", "tensor"), None)
    return jax.shard_map(
        functools.partial(local, mesh.shape["dp"], mesh.shape["tensor"]),
        mesh=mesh,
        in_specs=(
            rows,
            P(),
            P(),
            P(),
            P(),
            P(None, None, "tensor"),
            P(None, "tensor"),
            P("tensor", None),
            P(None, "tensor"),
            P("tensor"),
            P("tensor", None),
            P(),
            rows,
            P("dp", None),
        ),
        out_specs=(
            rows,
            rows,
            P(),
            P(),
            P(),
            P(),
            P(None, None, "tensor"),
            P(None, "tensor"),
            P("tensor", None),
            P(None, "tensor"),
            P("tensor"),
            P("tensor", None),
            P(),
        ),
        check_vma=False,
    )
```

```python
import functools
import math

import jax
import jax.numpy as jnp
from jax import lax
from jax.experimental import pallas as pl
from jax.experimental.pallas import tpu as pltpu
from jax.sharding import PartitionSpec as P

HD = 64
ROT = 16
MAXLEN = 512
EPSILON = 1e-05
MASKED_SCORE = -1e30
SQRT_HALF = 0.7071067811865476
INV_ROOT_TWO_PI = 0.3989422804014327
F32 = jnp.float32
BF16 = jnp.bfloat16
PAIR = 2 * HD
FIRST = 1
QROWS = 256
ROWS = 512
HIDDEN = 256
VMEM = 56 * 1024 * 1024


def dot(lhs, rhs, contract):
    return lax.dot_general(lhs, rhs, (contract, ((), ())), preferred_element_type=F32)


NN = ((1,), (0,))
NT = ((1,), (1,))
TN = ((0,), (0,))


ANY = pl.BlockSpec(memory_space=pl.ANY)
PARAMS = pltpu.CompilerParams(vmem_limit_bytes=VMEM)


def after(kernel, inputs, held):
    def body(*refs):
        kernel(*refs[:inputs], *refs[inputs + held :])

    return body


def prep_kernel(slot_ref, own_ref, other_ref, own_cot_ref, other_cot_ref, g1_ref, b1_ref, g2_ref, b2_ref,
                first_ref, second_ref, cot_ref):
    def emit(x_ref, c_ref):
        normed, _ = normalize(x_ref[...].astype(F32))
        first_ref[...] = (normed * g1_ref[...] + b1_ref[...]).astype(BF16)
        second_ref[...] = (normed * g2_ref[...] + b2_ref[...]).astype(BF16)
        cot_ref[...] = c_ref[...]

    pl.when(pl.program_id(0) == 0)(lambda: emit(own_ref, own_cot_ref))
    pl.when(pl.program_id(0) == 1)(lambda: emit(other_ref, other_cot_ref))


def prep(own, other, own_cot, other_cot, here, gains):
    rows, width = own.shape
    block = min(rows, 256)
    count = rows // block
    mine = pl.BlockSpec((block, width), lambda j, i, slot: (jnp.where(j == 0, i, count - 1), 0))
    theirs = pl.BlockSpec((block, width), lambda j, i, slot: (jnp.where(j == 0, 0, i), 0))
    vector = pl.BlockSpec((1, width), lambda j, i, slot: (0, 0))
    out = pl.BlockSpec((block, width), lambda j, i, slot: (slot[j] * count + i, 0))
    return pl.pallas_call(
        prep_kernel,
        grid_spec=pltpu.PrefetchScalarGridSpec(
            num_scalar_prefetch=1,
            grid=(2, count),
            in_specs=[mine, theirs, mine, theirs] + [vector] * 4,
            out_specs=[out] * 3,
        ),
        out_shape=[
            jax.ShapeDtypeStruct((2 * rows, width), BF16),
            jax.ShapeDtypeStruct((2 * rows, width), BF16),
            jax.ShapeDtypeStruct((2 * rows, width), BF16),
        ],
        compiler_params=PARAMS,
        cost_estimate=pl.CostEstimate(flops=rows * width * 40, bytes_accessed=rows * width * 20, transcendentals=0),
    )(jnp.stack([here, 1 - here]), own, other, own_cot, other_cot, *[g.reshape(1, -1) for g in gains])


def ffn_kernel(at_ref, second_ref, cot_ref, inner_ref, bias_ref, outer_ref, active_ref, back_ref, biasgrad_ref, *out_refs):
    second = second_ref[...]
    cot = cot_ref[...]
    preact = dot(second, inner_ref[...], NN) + bias_ref[...]
    cdf = 0.5 * (1.0 + lax.erf(preact * SQRT_HALF))
    slope = cdf + preact * jnp.exp(-0.5 * preact * preact) * INV_ROOT_TWO_PI
    active = (preact * cdf).astype(BF16)
    active_ref[...] = active
    pre_grad = dot(cot, outer_ref[...], NT) * slope
    biasgrad_ref[...] = jnp.sum(pre_grad, axis=0, keepdims=True)
    back = pre_grad.astype(BF16)
    back_ref[...] = back
    inner_grad = dot(second, back, TN)
    outer_grad = dot(active, cot, TN)
    if len(out_refs) == 4:
        left_away, left_own, right_away, right_own = out_refs
        half, cols = left_own.shape[0], right_own.shape[1]
        low, high = inner_grad[:half].astype(BF16), inner_grad[half:].astype(BF16)
        left_first = at_ref[0] == 0
        left_away[...] = jnp.where(left_first, high, low)
        left_own[...] = jnp.where(left_first, low, high)
        low, high = outer_grad[:, :cols].astype(BF16), outer_grad[:, cols:].astype(BF16)
        right_first = at_ref[1] == 0
        right_away[...] = jnp.where(right_first, high, low)
        right_own[...] = jnp.where(right_first, low, high)
    else:
        left_ref, right_ref = out_refs
        left_ref[...] = inner_grad.astype(BF16)
        cols = right_ref.shape[2]
        for c in range(right_ref.shape[0]):
            right_ref[c] = outer_grad[:, c * cols : (c + 1) * cols].astype(BF16)


def ffn_slice(second_in, cot, inner_weight, inner_bias, outer_weight, first, count, fast, mid, held=()):
    rows, width = second_in.shape
    cols = count * HIDDEN
    whole = pl.BlockSpec((rows, width), lambda j, at: (0, 0))
    split = fast[1] == 2 and mid[1] == 2 and width == 2 * cols
    out_specs = [
        pl.BlockSpec((rows, HIDDEN), lambda j, at: (0, j)),
        pl.BlockSpec((rows, HIDDEN), lambda j, at: (0, j)),
        pl.BlockSpec((1, HIDDEN), lambda j, at: (0, j)),
    ]
    out_shape = [
        jax.ShapeDtypeStruct((rows, cols), BF16),
        jax.ShapeDtypeStruct((rows, cols), BF16),
        jax.ShapeDtypeStruct((1, cols), F32),
    ]
    if split:
        out_specs += [pl.BlockSpec((cols, HIDDEN), lambda j, at: (0, j))] * 2
        out_specs += [pl.BlockSpec((HIDDEN, cols), lambda j, at: (j, 0))] * 2
        out_shape += [jax.ShapeDtypeStruct((cols, cols), BF16)] * 4
    else:
        out_specs += [
            pl.BlockSpec((width, HIDDEN), lambda j, at: (0, j)),
            pl.BlockSpec((width // cols, HIDDEN, cols), lambda j, at: (0, j, 0)),
        ]
        out_shape += [
            jax.ShapeDtypeStruct((width, cols), BF16),
            jax.ShapeDtypeStruct((width // cols, cols, cols), BF16),
        ]
    active, back, bias_grad, *grads = pl.pallas_call(
        after(ffn_kernel, 6, len(held)),
        grid_spec=pltpu.PrefetchScalarGridSpec(
            num_scalar_prefetch=1,
            grid=(count,),
            in_specs=[
                whole,
                whole,
                pl.BlockSpec((width, HIDDEN), lambda j, at: (0, first + j)),
                pl.BlockSpec((1, HIDDEN), lambda j, at: (0, first + j)),
                pl.BlockSpec((HIDDEN, width), lambda j, at: (first + j, 0)),
            ]
            + [ANY] * len(held),
            out_specs=out_specs,
        ),
        out_shape=out_shape,
        compiler_params=PARAMS,
        cost_estimate=pl.CostEstimate(
            flops=8 * rows * width * cols, bytes_accessed=20 * width * cols, transcendentals=2 * rows * cols
        ),
    )(jnp.stack([position(fast), position(mid)]), second_in, cot, inner_weight, inner_bias, outer_weight, *held)
    if split:
        return active, back, bias_grad, tuple(grads[:2]), tuple(grads[2:])
    return active, back, bias_grad, grads[0], grads[1].reshape(width, cols)


def partner(values):
    half = ROT // 2
    lane = lax.broadcasted_iota(jnp.int32, values.shape, 1) % HD
    lanes = values.shape[1]
    return jnp.where(lane < half, pltpu.roll(values, lanes - half, 1), pltpu.roll(values, half, 1))


def attention_kernel(
    slots, first_ref, cot_ref, w_ref, wbias_ref, dense_ref, cos_ref, sin_ref, segq_ref, segk_ref,
    context_ref, back_ref, grads_ref, dense_grads_ref, biasgrad_ref, mask_ref, dk_ref, dv_ref,
):
    rows = first_ref.shape[0]
    blocks = rows // QROWS
    reach = -(-(MAXLEN - 1) // QROWS)

    @pl.when(pl.program_id(0) == 0)
    def _():
        for i in range(blocks):
            low = max(0, i - reach) * QROWS
            span = (i + 1) * QROWS - low
            seg_q = segq_ref[i * QROWS : (i + 1) * QROWS, :]
            seg_k = segk_ref[:, low : low + span]
            q_at = lax.broadcasted_iota(jnp.int32, (QROWS, span), 0) + i * QROWS
            k_at = lax.broadcasted_iota(jnp.int32, (QROWS, span), 1) + low
            allowed = ((seg_q == seg_k) & (k_at <= q_at) & (seg_q < slots)) | (k_at == q_at)
            mask_ref[i * QROWS : (i + 1) * QROWS, :span] = jnp.where(allowed, 0.0, MASKED_SCORE)

    first = first_ref[...]
    cot = cot_ref[...]
    weight = jnp.concatenate([w_ref[0], w_ref[1], w_ref[2]], axis=1)
    bias = jnp.concatenate([wbias_ref[0], wbias_ref[1], wbias_ref[2]], axis=1)
    projected = dot(first, weight, NN) + bias
    cosine = cos_ref[...]
    sine = sin_ref[...]
    q = projected[:, :PAIR]
    k = projected[:, PAIR : 2 * PAIR]
    queries = (q * cosine + partner(q) * sine).astype(BF16)
    keys = (k * cosine + partner(k) * sine).astype(BF16)
    values = projected[:, 2 * PAIR :].astype(BF16)
    context_back = dot(cot, dense_ref[...], NT).astype(BF16)

    lane_head = lax.broadcasted_iota(jnp.int32, (QROWS, PAIR), 1) // HD
    scale = HD**-0.5
    dk_ref[...] = jnp.zeros_like(dk_ref)
    dv_ref[...] = jnp.zeros_like(dv_ref)
    contexts = []
    dqs = []
    for i in range(blocks):
        low = max(0, i - reach) * QROWS
        high = (i + 1) * QROWS
        mask = mask_ref[i * QROWS : high, : high - low]
        q_block = queries[i * QROWS : high]
        b_block = context_back[i * QROWS : high]
        k_block = keys[low:high]
        v_block = values[low:high]
        ctx = None
        for h in range(2):
            mine = lane_head == h
            q_head = jnp.where(mine, q_block, jnp.zeros_like(q_block))
            b_head = jnp.where(mine, b_block, jnp.zeros_like(b_block))
            scores = dot(q_head, k_block, NT) * scale + mask
            highest = jnp.max(scores, axis=1, keepdims=True)
            exponent = jnp.exp(scores - highest)
            total = jnp.sum(exponent, axis=1, keepdims=True)
            weights = exponent * (1.0 / total)
            weights_bf = weights.astype(BF16)
            prob_grad = dot(b_head, v_block, NT)
            delta = jnp.sum(weights * prob_grad, axis=1, keepdims=True)
            score_back = (weights * (prob_grad - delta)).astype(BF16)
            ctx_head = dot(weights_bf, v_block, NN)
            dq_head = dot(score_back, k_block, NN)
            dk_ref[low:high, :] += dot(score_back, q_head, TN)
            dv_ref[low:high, :] += dot(weights_bf, b_head, TN)
            ctx = ctx_head if h == 0 else jnp.where(mine, ctx_head, ctx)
            dq = dq_head if h == 0 else jnp.where(mine, dq_head, dq)
        contexts.append(ctx.astype(BF16))
        dqs.append(dq)
    context = jnp.concatenate(contexts, axis=0)
    context_ref[...] = context
    dq = jnp.concatenate(dqs, axis=0) * scale
    dk = dk_ref[...] * scale
    dv = dv_ref[...]
    dq = dq * cosine - partner(dq) * sine
    dk = dk * cosine - partner(dk) * sine
    back = jnp.concatenate([dq, dk, dv], axis=1)
    biasgrad_ref[...] = jnp.sum(back, axis=0, keepdims=True)
    back = back.astype(BF16)
    back_ref[...] = back
    weight_grad = dot(first, back, TN).astype(BF16)
    for c in range(3):
        grads_ref[c] = weight_grad[:, c * PAIR : (c + 1) * PAIR]
    dense_grads_ref[...] = dot(context, cot, TN).astype(BF16)


def attention_pair(first_in, cot, qkv, qkv_bias, dense_weight, cosine, sine, segment, slots, at, held=()):
    rows, width = first_in.shape
    reach = -(-(MAXLEN - 1) // QROWS)
    span = min(rows, (reach + 1) * QROWS)
    whole = pl.BlockSpec((rows, width), lambda j: (0, 0))
    table = pl.BlockSpec((rows, PAIR), lambda j: (0, 0))
    return pl.pallas_call(
        after(functools.partial(attention_kernel, slots), 9, len(held)),
        grid=(1,),
        in_specs=[
            whole,
            whole,
            pl.BlockSpec((3, width, PAIR), lambda j: (0, 0, at)),
            pl.BlockSpec((3, 1, PAIR), lambda j: (0, 0, at)),
            pl.BlockSpec((PAIR, width), lambda j: (at, 0)),
            table,
            table,
            pl.BlockSpec((rows, 1), lambda j: (0, 0)),
            pl.BlockSpec((1, rows), lambda j: (0, 0)),
        ]
        + [ANY] * len(held),
        out_specs=[
            pl.BlockSpec((rows, PAIR), lambda j: (0, 0)),
            pl.BlockSpec((rows, 3 * PAIR), lambda j: (0, 0)),
            pl.BlockSpec((3, width, PAIR), lambda j: (0, 0, 0)),
            pl.BlockSpec((PAIR, width), lambda j: (0, 0)),
            pl.BlockSpec((1, 3 * PAIR), lambda j: (0, 0)),
        ],
        out_shape=[
            jax.ShapeDtypeStruct((rows, PAIR), BF16),
            jax.ShapeDtypeStruct((rows, 3 * PAIR), BF16),
            jax.ShapeDtypeStruct((3, width, PAIR), BF16),
            jax.ShapeDtypeStruct((PAIR, width), BF16),
            jax.ShapeDtypeStruct((1, 3 * PAIR), F32),
        ],
        scratch_shapes=[
            pltpu.VMEM((rows, span), F32),
            pltpu.VMEM((rows, PAIR), F32),
            pltpu.VMEM((rows, PAIR), F32),
        ],
        compiler_params=PARAMS,
        cost_estimate=pl.CostEstimate(
            flops=30 * rows * width * PAIR,
            bytes_accessed=16 * width * PAIR,
            transcendentals=2 * rows * span,
        ),
    )(first_in, cot, qkv, qkv_bias, dense_weight, cosine, sine, segment.reshape(rows, 1), segment.reshape(1, rows), *held)


def branch_kernel(contexts, actives, slot_ref, *refs):
    context = jnp.concatenate([r[...] for r in refs[:contexts]], axis=1)
    active = jnp.concatenate([r[...] for r in refs[contexts : contexts + actives]], axis=1)
    dense_ref, outer_ref, away_ref, own_ref = refs[contexts + actives :]
    branch = (dot(context, dense_ref[...], NN) + dot(active, outer_ref[...], NN)).astype(BF16)

    @pl.when(pl.program_id(0) == 0)
    def _():
        away_ref[...] = branch

    @pl.when(pl.program_id(0) == 1)
    def _():
        own_ref[...] = branch


def back_kernel(qkv_backs, pre_backs, slot_ref, *refs):
    lanes = refs[:qkv_backs]
    pre_back = jnp.concatenate([r[...] for r in refs[qkv_backs : qkv_backs + pre_backs]], axis=1)
    qkv_ref, inner_ref, g1_ref, g2_ref, away_rows_ref, own_rows_ref, away_ref, own_ref, sums_ref = refs[qkv_backs + pre_backs :]
    first = None
    for c in range(3):
        part = jnp.concatenate([r[:, c * PAIR : (c + 1) * PAIR] for r in lanes], axis=1)
        term = dot(part, qkv_ref[c], NT)
        first = term if first is None else first + term
    second = dot(pre_back, inner_ref[...], NT)
    combined = first * g1_ref[...] + second * g2_ref[...]
    normed, _ = normalize(jnp.where(pl.program_id(0) == 0, away_rows_ref[...], own_rows_ref[...]).astype(F32))
    sums = jnp.concatenate(
        [jnp.sum(v, axis=0, keepdims=True) for v in (first * normed, first, second * normed, second)], axis=0
    )

    @pl.when((pl.program_id(0) == 0) & (pl.program_id(1) == 0))
    def _():
        sums_ref[...] = jnp.zeros_like(sums_ref)

    sums_ref[...] += sums

    @pl.when(pl.program_id(0) == 0)
    def _():
        away_ref[...] = combined.astype(BF16)

    @pl.when(pl.program_id(0) == 1)
    def _():
        own_ref[...] = combined


def rows_call(kernel, here, sliced, whole, halves, own_type, sums, held, flops):
    rows = sliced[0].shape[0]
    width = whole[0].shape[-1] if whole[0].ndim == 2 else whole[0].shape[1]
    half = rows // 2
    block = min(half, ROWS)
    count = half // block
    at = lambda j, i, slot: (slot[j] * count + i, 0)
    in_specs = [pl.BlockSpec((block, v.shape[1]), at) for v in sliced]
    in_specs += [pl.BlockSpec(v.shape, lambda j, i, slot, n=v.ndim: (0,) * n) for v in whole]
    by_half = [
        pl.BlockSpec((block, width), lambda j, i, slot: (jnp.where(j == 0, i, count - 1), 0)),
        pl.BlockSpec((block, width), lambda j, i, slot: (jnp.where(j == 0, 0, i), 0)),
    ]
    in_specs += by_half[: len(halves)]
    out_specs = list(by_half)
    out_shape = [jax.ShapeDtypeStruct((half, width), BF16), jax.ShapeDtypeStruct((half, width), own_type)]
    if sums:
        out_specs.append(pl.BlockSpec((sums, width), lambda j, i, slot: (0, 0)))
        out_shape.append(jax.ShapeDtypeStruct((sums, width), F32))
    return pl.pallas_call(
        after(kernel, 1 + len(in_specs), len(held)),
        grid_spec=pltpu.PrefetchScalarGridSpec(
            num_scalar_prefetch=1, grid=(2, count), in_specs=in_specs + [ANY] * len(held), out_specs=out_specs
        ),
        out_shape=out_shape,
        compiler_params=PARAMS,
        cost_estimate=pl.CostEstimate(flops=flops, bytes_accessed=16 * rows * width, transcendentals=0),
    )(jnp.stack([1 - here, here]), *sliced, *whole, *halves, *held)


def rings(size):
    fast = 2 if size % 2 == 0 else 1
    mid = 4 if size % 32 == 0 else 2 if size % 4 == 0 else 1
    return [(fast * mid, size // (fast * mid)), (fast, mid), (1, fast)]


def position(ring):
    return lax.axis_index("dp") // ring[0] % ring[1]


def hop(values, size, ring):
    stride, length = ring
    pairs = [(i, i + ((i // stride + 1) % length - i // stride % length) * stride) for i in range(size)]
    return lax.ppermute(values, "dp", pairs)


def rows_of(values, index, length):
    rows = values.shape[0] // length
    return lax.dynamic_slice_in_dim(values, index * rows, rows, 0)


def add(came, own):
    return (came.astype(F32) + own.astype(F32)).astype(BF16)


def ring_reduce(values, size, ring):
    length = ring[1]
    if isinstance(values, tuple):
        yield [values[0]]
        return add(hop(values[0], size, ring), values[1])
    if length == 1:
        return values
    at = position(ring)
    held = rows_of(values, (at + length - 1) % length, length)
    for step in range(length - 1):
        yield [held]
        came = hop(held, size, ring)
        held = add(came, rows_of(values, (at + 2 * length - 2 - step) % length, length))
    return held


def ring_pieces(held, size, ring):
    pieces = [held]
    for _ in range(ring[1] - 1):
        yield [pieces[-1]]
        pieces.append(hop(pieces[-1], size, ring))
    return pieces


def slots_of(ring):
    at = position(ring)
    return [(at + ring[1] - back) % ring[1] for back in range(ring[1])]


def join(pieces, ring):
    slots = slots_of(ring)
    ordered = []
    for slot in range(ring[1]):
        chosen = pieces[0]
        for back in range(1, ring[1]):
            chosen = jnp.where(slots[back] == slot, pieces[back], chosen)
        ordered.append(chosen)
    return jnp.concatenate(ordered, axis=0)


def together(one, two):
    results = [None, None]
    live = [one, two]
    while any(g is not None for g in live):
        held = []
        for k, g in enumerate(live):
            if g is None:
                continue
            try:
                held += next(g)
            except StopIteration as stop:
                results[k] = stop.value
                live[k] = None
        if held:
            yield held
    return results


def reduce_over_dp(left, right, size):
    slow, mid, fast = rings(size)
    left, right = yield from together(ring_reduce(left, size, fast), ring_reduce(right, size, mid))
    left, right = yield from together(ring_reduce(left, size, mid), ring_reduce(right, size, fast))
    both = jnp.stack([left, right])
    step = 1
    while step < slow[1]:
        yield [both]
        both = add(lax.ppermute(both, "dp", [(i, i ^ (step * slow[0])) for i in range(size)]), both)
        step *= 2
    left, right = yield from together(ring_pieces(both[0], size, mid), ring_pieces(both[1], size, fast))
    left, right = join(left, mid), join(right, fast)
    return (yield from together(ring_pieces(left, size, fast), ring_pieces(right, size, mid)))


def place_kernel(lefts, rights, kept, left_ref, right_ref, *refs):
    pieces, (inner_ref, outer_ref, token_ref) = refs[: lefts + rights], refs[lefts + rights + kept :]
    step = pl.program_id(0)
    for k in range(lefts):

        @pl.when(step == k)
        def _():
            inner_ref[...] = pieces[k][...].astype(F32)

    for k in range(rights):

        @pl.when(step == k)
        def _():
            outer_ref[...] = pieces[lefts + k][...].astype(F32)

    token_ref[...] = jnp.zeros_like(token_ref)


def place(totals, shapes, left, right, fast, mid, at):
    cuts = 2
    steps = max(len(left), len(right))
    rows, cols = left[0].shape
    tall, wide = right[0].shape

    def taken(k, count):
        return lambda j, i, a, b: (jnp.where(j == k, i, jnp.where(j < k, 0, cuts - 1)), 0)

    def last(j, i, count):
        return jnp.minimum(j, count - 1), jnp.where(j < count, i, cuts - 1)

    def left_at(j, i, a, b):
        j, i = last(j, i, len(left))
        return a[j] * cuts + i, at

    def right_at(j, i, a, b):
        j, i = last(j, i, len(right))
        return at * cuts + i, b[j]

    kept = list(totals) if totals else []
    return pl.pallas_call(
        functools.partial(place_kernel, len(left), len(right), len(kept)),
        grid_spec=pltpu.PrefetchScalarGridSpec(
            num_scalar_prefetch=2,
            grid=(steps, cuts),
            in_specs=[pl.BlockSpec((rows // cuts, cols), taken(k, len(left))) for k in range(len(left))]
            + [pl.BlockSpec((tall // cuts, wide), taken(k, len(right))) for k in range(len(right))]
            + [ANY] * len(kept),
            out_specs=[
                pl.BlockSpec((rows // cuts, cols), left_at),
                pl.BlockSpec((tall // cuts, wide), right_at),
                pl.BlockSpec((8, 128), lambda j, i, a, b: (0, 0)),
            ],
        ),
        out_shape=[jax.ShapeDtypeStruct(shape, F32) for shape in shapes] + [jax.ShapeDtypeStruct((8, 128), F32)],
        input_output_aliases={2 + len(left) + len(right) + k: k for k in range(len(kept))},
        compiler_params=PARAMS,
        cost_estimate=pl.CostEstimate(flops=0, bytes_accessed=12 * len(left) * rows * cols, transcendentals=0),
    )(jnp.stack(slots_of(fast)), jnp.stack(slots_of(mid)), *left, *right, *kept)


def butterfly(values, axis, size):
    if size & (size - 1):
        return lax.psum(values, axis)
    step = 1
    while step < size:
        values = values + lax.ppermute(values, axis, [(i, i ^ step) for i in range(size)])
        step *= 2
    return values


class Rounds:
    def __init__(self, finish):
        self.live = []
        self.finish = finish
        self.block = []

    def add(self, at, steps):
        self.live.append((at, steps))

    def turn(self):
        held = self.block
        left = []
        for at, steps in self.live:
            try:
                held = held + next(steps)
                left.append((at, steps))
            except StopIteration as stop:
                held = held + [self.finish(at, *stop.value)]
        self.live = left
        return held


def normalize(values):
    mean_val = jnp.mean(values, axis=-1, keepdims=True)
    centred = values - mean_val
    inv_std = lax.rsqrt(jnp.mean(centred * centred, axis=-1, keepdims=True) + EPSILON)
    return (centred * inv_std, inv_std)


def layout(lengths, row_count):
    slot_count = lengths.shape[0]
    places = jnp.arange(row_count, dtype=jnp.int32)
    seq_ends = jnp.cumsum(lengths)
    seq_starts = seq_ends - lengths
    segment = jnp.sum((places[:, None] >= seq_ends[None, :]).astype(jnp.int32), axis=1)
    member = segment[:, None] == jnp.arange(slot_count, dtype=jnp.int32)[None, :]
    place = places - jnp.sum(jnp.where(member, seq_starts[None, :], 0), axis=1)
    return (segment, place)


def rotary_tables(places):
    half = ROT // 2
    lane = jnp.arange(PAIR, dtype=jnp.int32) % HD
    frequency = jnp.exp(-(2.0 * (lane % half).astype(F32) / ROT) * math.log(10000.0))
    angle = places.astype(F32)[:, None] * jnp.where(lane < ROT, frequency, 0.0)[None, :]
    sign = jnp.where(lane < half, -1.0, jnp.where(lane < ROT, 1.0, 0.0))
    return (jnp.cos(angle), jnp.sin(angle) * sign[None, :])


def local(
    dp_size,
    tensor_size,
    residual,
    norm1_gain,
    norm1_bias,
    norm2_gain,
    norm2_bias,
    qkv_weight,
    qkv_bias,
    dense_weight,
    inner_weight,
    inner_bias,
    outer_weight,
    out_bias,
    cotangent,
    seq_lengths,
):
    width = residual.shape[1]
    head_width = qkv_weight.shape[2]
    hidden = inner_weight.shape[1]
    slots = seq_lengths.shape[1]
    here = lax.axis_index("tensor")
    swap = [(0, 1), (1, 0)]

    if tensor_size == 2:
        other = lax.ppermute(residual, "tensor", swap)
        other_cot = lax.ppermute(cotangent, "tensor", swap)
        parts = (residual, other, cotangent, other_cot)
        order = here
        row_halves = [other, residual]
    else:
        gathered = lax.all_gather(residual, "tensor", axis=0, tiled=True)
        gathered_cot = lax.all_gather(cotangent, "tensor", axis=0, tiled=True)
        middle = gathered.shape[0] // 2
        parts = (gathered[:middle], gathered[middle:], gathered_cot[:middle], gathered_cot[middle:])
        row_halves = list(parts[:2])
        order = jnp.int32(0)
    first_in, second_in, cot = prep(*parts, order, (norm1_gain, norm1_bias, norm2_gain, norm2_bias))
    rows = cot.shape[0]

    _, mid, fast = rings(dp_size)
    totals = []

    def finish(at, left, right):
        inner, outer, token = place(totals, [(width, hidden), (hidden, width)], left, right, fast, mid, at)
        totals[:] = [inner, outer]
        return token

    rounds = Rounds(finish)
    ffn = []
    attn = []
    steps = hidden // HIDDEN
    per = max(1, steps // 4)

    def feed_forward():
        out = ffn_slice(
            second_in, cot, inner_weight, inner_bias.reshape(1, -1), outer_weight, len(ffn) * per, per, fast, mid,
            rounds.turn(),
        )
        rounds.block = [out[2]]
        rounds.add(len(ffn), reduce_over_dp(out[3], out[4], dp_size))
        ffn.append(out)

    for _ in range(FIRST):
        feed_forward()
    segment, places = layout(seq_lengths[0], rows)
    cosine, sine = rotary_tables(places)
    qkv = jnp.transpose(qkv_weight, (1, 0, 2))
    for pair in range(head_width // PAIR):
        out = attention_pair(
            first_in, cot, qkv, qkv_bias.reshape(3, 1, -1), dense_weight, cosine, sine, segment, slots, pair,
            rounds.turn(),
        )
        rounds.block = [out[4]]
        attn.append(out)
    attn_sums = lax.psum(([a[2] for a in attn], [a[3] for a in attn]), "dp")
    while len(ffn) * per < steps:
        feed_forward()

    order = here if tensor_size == 2 else jnp.int32(1)
    held = rounds.turn()
    branch_away, branch_own = rows_call(
        functools.partial(branch_kernel, len(attn), len(ffn)), order, [a[0] for a in attn] + [f[0] for f in ffn],
        [dense_weight, outer_weight], [], BF16, 0, held, 2 * rows * width * (head_width + hidden),
    )
    rounds.block = []
    held = rounds.turn() + [branch_away]
    away, own, sums = rows_call(
        functools.partial(back_kernel, len(attn), len(ffn)), order, [a[1] for a in attn] + [f[1] for f in ffn],
        [qkv, inner_weight, norm1_gain.reshape(1, -1), norm2_gain.reshape(1, -1)], row_halves, F32, 4, held,
        2 * rows * width * (3 * head_width + hidden),
    )
    if tensor_size == 2:
        summed = lax.ppermute(branch_away, "tensor", swap).astype(F32) + branch_own.astype(F32)
        combined = lax.ppermute(away, "tensor", swap).astype(F32) + own
    else:
        scatter = functools.partial(lax.psum_scatter, axis_name="tensor", scatter_dimension=0, tiled=True)
        summed = scatter(jnp.concatenate([branch_away, branch_own], axis=0)).astype(F32)
        combined = scatter(jnp.concatenate([away.astype(F32), own], axis=0))
    layer_out = (residual.astype(F32) + summed + out_bias).astype(BF16)
    own_normed, own_inv = normalize(residual.astype(F32))
    residual_grad = (
        cotangent.astype(F32)
        + own_inv
        * (
            combined
            - jnp.mean(combined, axis=-1, keepdims=True)
            - own_normed * jnp.mean(combined * own_normed, axis=-1, keepdims=True)
        )
    ).astype(BF16)

    over_all = jnp.concatenate([sums, jnp.sum(cotangent.astype(F32), axis=0, keepdims=True)], axis=0).reshape(-1)
    over_all = butterfly(over_all, "tensor", tensor_size)
    qkvbias = jnp.concatenate([a[4].reshape(3, PAIR) for a in attn], axis=1).reshape(-1)
    innerbias = jnp.concatenate([f[2] for f in ffn], axis=1).reshape(-1)
    vectors = butterfly(jnp.concatenate([over_all, qkvbias, innerbias]), "dp", dp_size)
    ends = [width * i for i in range(1, 6)] + [5 * width + 3 * head_width]
    gain1_grad, bias1_grad, gain2_grad, bias2_grad, outbias_grad, qkvbias_grad, innerbias_grad = jnp.split(vectors, ends)

    while rounds.live:
        rounds.turn()
    inner_grad, outer_grad = totals
    qkv_sums, dense_sums = attn_sums
    qkv_grad = jnp.concatenate([g.transpose(1, 0, 2) for g in qkv_sums], axis=2).astype(F32)
    dense_grad = jnp.concatenate(dense_sums, axis=0).astype(F32)
    return (
        layer_out,
        residual_grad,
        gain1_grad,
        bias1_grad,
        gain2_grad,
        bias2_grad,
        qkv_grad,
        qkvbias_grad.reshape(3, head_width),
        dense_grad,
        inner_grad,
        innerbias_grad,
        outer_grad,
        outbias_grad,
    )


def solution(mesh):
    rows = P(("dp", "tensor"), None)
    return jax.shard_map(
        functools.partial(local, mesh.shape["dp"], mesh.shape["tensor"]),
        mesh=mesh,
        in_specs=(
            rows,
            P(),
            P(),
            P(),
            P(),
            P(None, None, "tensor"),
            P(None, "tensor"),
            P("tensor", None),
            P(None, "tensor"),
            P("tensor"),
            P("tensor", None),
            P(),
            rows,
            P("dp", None),
        ),
        out_specs=(
            rows,
            rows,
            P(),
            P(),
            P(),
            P(),
            P(None, None, "tensor"),
            P(None, "tensor"),
            P("tensor", None),
            P(None, "tensor"),
            P("tensor"),
            P("tensor", None),
            P(),
        ),
        check_vma=False,
    )
```

```python
import functools
import math

import jax
import jax.numpy as jnp
from jax import lax
from jax.experimental import pallas as pl
from jax.experimental.pallas import tpu as pltpu
from jax.sharding import Mesh
from jax.sharding import PartitionSpec as P

HD = 64
ROT = 16
MAXLEN = 512
EPSILON = 1e-05
MASKED_SCORE = -1e30
SQRT_HALF = 0.7071067811865476
INV_ROOT_TWO_PI = 0.3989422804014327
F32 = jnp.float32
BF16 = jnp.bfloat16
PAIR = 2 * HD
CHUNK_PAIRS = 2
QROWS = 256
ROWS = 512
HIDDEN = 256
VMEM = 56 * 1024 * 1024


def dot(lhs, rhs, contract):
    return lax.dot_general(lhs, rhs, (contract, ((), ())), preferred_element_type=F32)


NN = ((1,), (0,))
NT = ((1,), (1,))
TN = ((0,), (0,))


ANY = pl.BlockSpec(memory_space=pl.ANY)
PARAMS = pltpu.CompilerParams(vmem_limit_bytes=VMEM)


def after(kernel, inputs, held):
    def body(*refs):
        kernel(*refs[:inputs], *refs[inputs + held :])

    return body


def prep_kernel(slot_ref, own_ref, other_ref, own_cot_ref, other_cot_ref, g1_ref, b1_ref, g2_ref, b2_ref,
                first_ref, second_ref, cot_ref):
    def emit(x_ref, c_ref):
        normed, _ = normalize(x_ref[...].astype(F32))
        first_ref[...] = (normed * g1_ref[...] + b1_ref[...]).astype(BF16)
        second_ref[...] = (normed * g2_ref[...] + b2_ref[...]).astype(BF16)
        cot_ref[...] = c_ref[...]

    pl.when(pl.program_id(0) == 0)(lambda: emit(own_ref, own_cot_ref))
    pl.when(pl.program_id(0) == 1)(lambda: emit(other_ref, other_cot_ref))


def prep(own, other, own_cot, other_cot, here, gains):
    rows, width = own.shape
    block = min(rows, 256)
    count = rows // block
    mine = pl.BlockSpec((block, width), lambda j, i, slot: (jnp.where(j == 0, i, count - 1), 0))
    theirs = pl.BlockSpec((block, width), lambda j, i, slot: (jnp.where(j == 0, 0, i), 0))
    vector = pl.BlockSpec((1, width), lambda j, i, slot: (0, 0))
    out = pl.BlockSpec((block, width), lambda j, i, slot: (slot[j] * count + i, 0))
    return pl.pallas_call(
        prep_kernel,
        grid_spec=pltpu.PrefetchScalarGridSpec(
            num_scalar_prefetch=1,
            grid=(2, count),
            in_specs=[mine, theirs, mine, theirs] + [vector] * 4,
            out_specs=[out] * 3,
        ),
        out_shape=[
            jax.ShapeDtypeStruct((2 * rows, width), BF16),
            jax.ShapeDtypeStruct((2 * rows, width), BF16),
            jax.ShapeDtypeStruct((2 * rows, width), BF16),
        ],
        compiler_params=PARAMS,
        cost_estimate=pl.CostEstimate(flops=rows * width * 40, bytes_accessed=rows * width * 20, transcendentals=0),
    )(jnp.stack([here, 1 - here]), own, other, own_cot, other_cot, *[g.reshape(1, -1) for g in gains])


def ffn_kernel(at_ref, second_ref, cot_ref, inner_ref, bias_ref, outer_ref, active_ref, back_ref, biasgrad_ref, *out_refs):
    second = second_ref[...]
    cot = cot_ref[...]
    preact = dot(second, inner_ref[...], NN) + bias_ref[...]
    cdf = 0.5 * (1.0 + lax.erf(preact * SQRT_HALF))
    slope = cdf + preact * jnp.exp(-0.5 * preact * preact) * INV_ROOT_TWO_PI
    active = (preact * cdf).astype(BF16)
    active_ref[...] = active
    pre_grad = dot(cot, outer_ref[...], NT) * slope
    biasgrad_ref[...] = jnp.sum(pre_grad, axis=0, keepdims=True)
    back = pre_grad.astype(BF16)
    back_ref[...] = back
    inner_grad = dot(second, back, TN)
    outer_grad = dot(active, cot, TN)
    if len(out_refs) == 4:
        left_away, left_own, right_away, right_own = out_refs
        half, cols = left_own.shape[0], right_own.shape[1]
        low, high = inner_grad[:half].astype(BF16), inner_grad[half:].astype(BF16)
        left_first = at_ref[0] == 0
        left_away[...] = jnp.where(left_first, high, low)
        left_own[...] = jnp.where(left_first, low, high)
        low, high = outer_grad[:, :cols].astype(BF16), outer_grad[:, cols:].astype(BF16)
        right_first = at_ref[1] == 0
        right_away[...] = jnp.where(right_first, high, low)
        right_own[...] = jnp.where(right_first, low, high)
    else:
        left_ref, right_ref = out_refs
        left_ref[...] = inner_grad.astype(BF16)
        cols = right_ref.shape[2]
        for c in range(right_ref.shape[0]):
            right_ref[c] = outer_grad[:, c * cols : (c + 1) * cols].astype(BF16)


def ffn_slice(second_in, cot, inner_weight, inner_bias, outer_weight, first, count, fast, mid, held=()):
    rows, width = second_in.shape
    cols = count * HIDDEN
    whole = pl.BlockSpec((rows, width), lambda j, at: (0, 0))
    split = fast[1] == 2 and mid[1] == 2
    out_specs = [
        pl.BlockSpec((rows, HIDDEN), lambda j, at: (0, j)),
        pl.BlockSpec((rows, HIDDEN), lambda j, at: (0, j)),
        pl.BlockSpec((1, HIDDEN), lambda j, at: (0, j)),
    ]
    out_shape = [
        jax.ShapeDtypeStruct((rows, cols), BF16),
        jax.ShapeDtypeStruct((rows, cols), BF16),
        jax.ShapeDtypeStruct((1, cols), F32),
    ]
    if split:
        out_specs += [pl.BlockSpec((width // 2, HIDDEN), lambda j, at: (0, j))] * 2
        out_specs += [pl.BlockSpec((HIDDEN, width // 2), lambda j, at: (j, 0))] * 2
        out_shape += [jax.ShapeDtypeStruct((width // 2, cols), BF16)] * 2
        out_shape += [jax.ShapeDtypeStruct((cols, width // 2), BF16)] * 2
    else:
        out_specs += [
            pl.BlockSpec((width, HIDDEN), lambda j, at: (0, j)),
            pl.BlockSpec((width // cols, HIDDEN, cols), lambda j, at: (0, j, 0)),
        ]
        out_shape += [
            jax.ShapeDtypeStruct((width, cols), BF16),
            jax.ShapeDtypeStruct((width // cols, cols, cols), BF16),
        ]
    active, back, bias_grad, *grads = pl.pallas_call(
        after(ffn_kernel, 6, len(held)),
        grid_spec=pltpu.PrefetchScalarGridSpec(
            num_scalar_prefetch=1,
            grid=(count,),
            in_specs=[
                whole,
                whole,
                pl.BlockSpec((width, HIDDEN), lambda j, at: (0, first + j)),
                pl.BlockSpec((1, HIDDEN), lambda j, at: (0, first + j)),
                pl.BlockSpec((HIDDEN, width), lambda j, at: (first + j, 0)),
            ]
            + [ANY] * len(held),
            out_specs=out_specs,
        ),
        out_shape=out_shape,
        compiler_params=PARAMS,
        cost_estimate=pl.CostEstimate(
            flops=8 * rows * width * cols, bytes_accessed=20 * width * cols, transcendentals=2 * rows * cols
        ),
    )(jnp.stack([position(fast), position(mid)]), second_in, cot, inner_weight, inner_bias, outer_weight, *held)
    if split:
        return active, back, bias_grad, tuple(grads[:2]), tuple(grads[2:])
    return active, back, bias_grad, grads[0], grads[1].reshape(width, cols)


def partner(values):
    half = ROT // 2
    lane = lax.broadcasted_iota(jnp.int32, values.shape, 1) % HD
    lanes = values.shape[1]
    return jnp.where(lane < half, pltpu.roll(values, lanes - half, 1), pltpu.roll(values, half, 1))


def attention_kernel(
    slots, split, at_ref, first_ref, cot_ref, w_ref, wbias_ref, dense_ref, cos_ref, sin_ref, segq_ref, segk_ref,
    context_ref, back_ref, biasgrad_ref, *refs,
):
    *out_refs, mask_ref, dk_ref, dv_ref = refs
    rows = first_ref.shape[0]
    blocks = rows // QROWS
    reach = -(-(MAXLEN - 1) // QROWS)

    @pl.when(pl.program_id(0) == 0)
    def _():
        for i in range(blocks):
            low = max(0, i - reach) * QROWS
            span = (i + 1) * QROWS - low
            seg_q = segq_ref[i * QROWS : (i + 1) * QROWS, :]
            seg_k = segk_ref[:, low : low + span]
            q_at = lax.broadcasted_iota(jnp.int32, (QROWS, span), 0) + i * QROWS
            k_at = lax.broadcasted_iota(jnp.int32, (QROWS, span), 1) + low
            allowed = ((seg_q == seg_k) & (k_at <= q_at) & (seg_q < slots)) | (k_at == q_at)
            mask_ref[i * QROWS : (i + 1) * QROWS, :span] = jnp.where(allowed, 0.0, MASKED_SCORE)

    first = first_ref[...]
    cot = cot_ref[...]
    weight = jnp.concatenate([w_ref[0], w_ref[1], w_ref[2]], axis=1)
    bias = jnp.concatenate([wbias_ref[0], wbias_ref[1], wbias_ref[2]], axis=1)
    projected = dot(first, weight, NN) + bias
    cosine = cos_ref[...]
    sine = sin_ref[...]
    q = projected[:, :PAIR]
    k = projected[:, PAIR : 2 * PAIR]
    queries = (q * cosine + partner(q) * sine).astype(BF16)
    keys = (k * cosine + partner(k) * sine).astype(BF16)
    values = projected[:, 2 * PAIR :].astype(BF16)
    context_back = dot(cot, dense_ref[...], NT).astype(BF16)

    lane_head = lax.broadcasted_iota(jnp.int32, (QROWS, PAIR), 1) // HD
    scale = HD**-0.5
    dk_ref[...] = jnp.zeros_like(dk_ref)
    dv_ref[...] = jnp.zeros_like(dv_ref)
    contexts = []
    dqs = []
    for i in range(blocks):
        low = max(0, i - reach) * QROWS
        high = (i + 1) * QROWS
        mask = mask_ref[i * QROWS : high, : high - low]
        q_block = queries[i * QROWS : high]
        b_block = context_back[i * QROWS : high]
        k_block = keys[low:high]
        v_block = values[low:high]
        ctx = None
        for h in range(2):
            mine = lane_head == h
            q_head = jnp.where(mine, q_block, jnp.zeros_like(q_block))
            b_head = jnp.where(mine, b_block, jnp.zeros_like(b_block))
            scores = dot(q_head, k_block, NT) * scale + mask
            highest = jnp.max(scores, axis=1, keepdims=True)
            exponent = jnp.exp(scores - highest)
            total = jnp.sum(exponent, axis=1, keepdims=True)
            weights = exponent * (1.0 / total)
            weights_bf = weights.astype(BF16)
            prob_grad = dot(b_head, v_block, NT)
            delta = jnp.sum(weights * prob_grad, axis=1, keepdims=True)
            score_back = (weights * (prob_grad - delta)).astype(BF16)
            ctx_head = dot(weights_bf, v_block, NN)
            dq_head = dot(score_back, k_block, NN)
            dk_ref[low:high, :] += dot(score_back, q_head, TN)
            dv_ref[low:high, :] += dot(weights_bf, b_head, TN)
            ctx = ctx_head if h == 0 else jnp.where(mine, ctx_head, ctx)
            dq = dq_head if h == 0 else jnp.where(mine, dq_head, dq)
        contexts.append(ctx.astype(BF16))
        dqs.append(dq)
    context = jnp.concatenate(contexts, axis=0)
    context_ref[...] = context
    dq = jnp.concatenate(dqs, axis=0) * scale
    dk = dk_ref[...] * scale
    dv = dv_ref[...]
    dq = dq * cosine - partner(dq) * sine
    dk = dk * cosine - partner(dk) * sine
    back = jnp.concatenate([dq, dk, dv], axis=1)
    biasgrad_ref[...] = jnp.sum(back, axis=0, keepdims=True)
    back = back.astype(BF16)
    back_ref[...] = back
    weight_grad = dot(first, back, TN).astype(BF16)
    dense_grad = dot(context, cot, TN).astype(BF16)
    if split:
        tiles = [dense_grad[:, c * PAIR : (c + 1) * PAIR] for c in range(dense_grad.shape[1] // PAIR)]
        right = jnp.concatenate([weight_grad[:, 2 * PAIR :], jnp.concatenate(tiles, axis=0)], axis=1)
        for side, grad in enumerate((weight_grad[:, : 2 * PAIR], right)):
            half = grad.shape[0] // 2
            first_half = at_ref[side] == 0
            out_refs[2 * side][...] = jnp.where(first_half, grad[half:], grad[:half])
            out_refs[2 * side + 1][...] = jnp.where(first_half, grad[:half], grad[half:])
    else:
        grads_ref, dense_grads_ref = out_refs
        for c in range(3):
            grads_ref[c] = weight_grad[:, c * PAIR : (c + 1) * PAIR]
        dense_grads_ref[...] = dense_grad


def attention_pair(
    first_in, cot, qkv, qkv_bias, dense_weight, cosine, sine, segment, slots, pair, fast, mid, chunk, place, held
):
    rows, width = first_in.shape
    reach = -(-(MAXLEN - 1) // QROWS)
    span = min(rows, (reach + 1) * QROWS)
    split = fast[1] == 2 and mid[1] == 2
    kept = list(chunk) if chunk else []

    def fixed(*shape):
        return pl.BlockSpec(shape, lambda j, at: (0,) * len(shape))

    out_specs = [fixed(rows, PAIR), fixed(rows, 3 * PAIR), fixed(1, 3 * PAIR)]
    out_shape = [
        jax.ShapeDtypeStruct((rows, PAIR), BF16),
        jax.ShapeDtypeStruct((rows, 3 * PAIR), BF16),
        jax.ShapeDtypeStruct((1, 3 * PAIR), F32),
    ]
    if split:
        out_specs += [pl.BlockSpec((width // 2, 2 * PAIR), lambda j, at: (0, place))] * 4
        out_shape += [jax.ShapeDtypeStruct((width // 2, 2 * PAIR * CHUNK_PAIRS), BF16)] * 4
    else:
        out_specs += [fixed(3, width, PAIR), fixed(PAIR, width)]
        out_shape += [jax.ShapeDtypeStruct((3, width, PAIR), BF16), jax.ShapeDtypeStruct((PAIR, width), BF16)]
    return pl.pallas_call(
        after(functools.partial(attention_kernel, slots, split), 10, len(held) + len(kept)),
        grid_spec=pltpu.PrefetchScalarGridSpec(
            num_scalar_prefetch=1,
            grid=(1,),
            in_specs=[
                fixed(rows, width),
                fixed(rows, width),
                pl.BlockSpec((3, width, PAIR), lambda j, at: (0, 0, pair)),
                pl.BlockSpec((3, 1, PAIR), lambda j, at: (0, 0, pair)),
                pl.BlockSpec((PAIR, width), lambda j, at: (pair, 0)),
                fixed(rows, PAIR),
                fixed(rows, PAIR),
                fixed(rows, 1),
                fixed(1, rows),
            ]
            + [ANY] * (len(held) + len(kept)),
            out_specs=out_specs,
            scratch_shapes=[
                pltpu.VMEM((rows, span), F32),
                pltpu.VMEM((rows, PAIR), F32),
                pltpu.VMEM((rows, PAIR), F32),
            ],
        ),
        out_shape=out_shape,
        input_output_aliases={10 + k: 3 + k for k in range(len(kept))},
        compiler_params=PARAMS,
        cost_estimate=pl.CostEstimate(
            flops=30 * rows * width * PAIR, bytes_accessed=16 * width * PAIR, transcendentals=2 * rows * span
        ),
    )(
        jnp.stack([position(fast), position(mid)]), first_in, cot, qkv, qkv_bias, dense_weight, cosine, sine,
        segment.reshape(rows, 1), segment.reshape(1, rows), *kept, *held,
    )


def branch_kernel(contexts, actives, slot_ref, *refs):
    context = jnp.concatenate([r[...] for r in refs[:contexts]], axis=1)
    active = jnp.concatenate([r[...] for r in refs[contexts : contexts + actives]], axis=1)
    dense_ref, outer_ref, away_ref, own_ref = refs[contexts + actives :]
    branch = (dot(context, dense_ref[...], NN) + dot(active, outer_ref[...], NN)).astype(BF16)

    @pl.when(pl.program_id(0) == 0)
    def _():
        away_ref[...] = branch

    @pl.when(pl.program_id(0) == 1)
    def _():
        own_ref[...] = branch


def back_kernel(qkv_backs, pre_backs, slot_ref, *refs):
    lanes = refs[:qkv_backs]
    pre_back = jnp.concatenate([r[...] for r in refs[qkv_backs : qkv_backs + pre_backs]], axis=1)
    qkv_ref, inner_ref, g1_ref, g2_ref, away_rows_ref, own_rows_ref, away_ref, own_ref, sums_ref = refs[qkv_backs + pre_backs :]
    first = None
    for c in range(3):
        part = jnp.concatenate([r[:, c * PAIR : (c + 1) * PAIR] for r in lanes], axis=1)
        term = dot(part, qkv_ref[c], NT)
        first = term if first is None else first + term
    second = dot(pre_back, inner_ref[...], NT)
    combined = first * g1_ref[...] + second * g2_ref[...]
    normed, _ = normalize(jnp.where(pl.program_id(0) == 0, away_rows_ref[...], own_rows_ref[...]).astype(F32))
    sums = jnp.concatenate(
        [jnp.sum(v, axis=0, keepdims=True) for v in (first * normed, first, second * normed, second)], axis=0
    )

    @pl.when((pl.program_id(0) == 0) & (pl.program_id(1) == 0))
    def _():
        sums_ref[...] = jnp.zeros_like(sums_ref)

    sums_ref[...] += sums

    @pl.when(pl.program_id(0) == 0)
    def _():
        away_ref[...] = combined.astype(BF16)

    @pl.when(pl.program_id(0) == 1)
    def _():
        own_ref[...] = combined


def rows_call(kernel, here, sliced, whole, halves, own_type, sums, held, flops):
    rows = sliced[0].shape[0]
    width = whole[0].shape[-1] if whole[0].ndim == 2 else whole[0].shape[1]
    half = rows // 2
    block = min(half, ROWS)
    count = half // block
    at = lambda j, i, slot: (slot[j] * count + i, 0)
    in_specs = [pl.BlockSpec((block, v.shape[1]), at) for v in sliced]
    in_specs += [pl.BlockSpec(v.shape, lambda j, i, slot, n=v.ndim: (0,) * n) for v in whole]
    by_half = [
        pl.BlockSpec((block, width), lambda j, i, slot: (jnp.where(j == 0, i, count - 1), 0)),
        pl.BlockSpec((block, width), lambda j, i, slot: (jnp.where(j == 0, 0, i), 0)),
    ]
    in_specs += by_half[: len(halves)]
    out_specs = list(by_half)
    out_shape = [jax.ShapeDtypeStruct((half, width), BF16), jax.ShapeDtypeStruct((half, width), own_type)]
    if sums:
        out_specs.append(pl.BlockSpec((sums, width), lambda j, i, slot: (0, 0)))
        out_shape.append(jax.ShapeDtypeStruct((sums, width), F32))
    return pl.pallas_call(
        after(kernel, 1 + len(in_specs), len(held)),
        grid_spec=pltpu.PrefetchScalarGridSpec(
            num_scalar_prefetch=1, grid=(2, count), in_specs=in_specs + [ANY] * len(held), out_specs=out_specs
        ),
        out_shape=out_shape,
        compiler_params=PARAMS,
        cost_estimate=pl.CostEstimate(flops=flops, bytes_accessed=16 * rows * width, transcendentals=0),
    )(jnp.stack([1 - here, here]), *sliced, *whole, *halves, *held)


def rings(size):
    fast = 2 if size % 2 == 0 else 1
    mid = 4 if size % 32 == 0 else 2 if size % 4 == 0 else 1
    return [(fast * mid, size // (fast * mid)), (fast, mid), (1, fast)]


DP = ("slow", "mid", "fast")


def position(ring):
    return lax.axis_index(DP) // ring[0] % ring[1]


def hop(values, size, ring):
    stride, length = ring
    pairs = [(i, i + ((i // stride + 1) % length - i // stride % length) * stride) for i in range(size)]
    return lax.ppermute(values, DP, pairs)


def rows_of(values, index, length):
    rows = values.shape[0] // length
    return lax.dynamic_slice_in_dim(values, index * rows, rows, 0)


def add(came, own):
    return (came.astype(F32) + own.astype(F32)).astype(BF16)


def ring_reduce(values, size, ring):
    length = ring[1]
    if isinstance(values, tuple):
        yield [values[0]]
        return add(hop(values[0], size, ring), values[1])
    if length == 1:
        return values
    at = position(ring)
    held = rows_of(values, (at + length - 1) % length, length)
    for step in range(length - 1):
        yield [held]
        came = hop(held, size, ring)
        held = add(came, rows_of(values, (at + 2 * length - 2 - step) % length, length))
    return held


def ring_pieces(held, size, ring):
    pieces = [held]
    for _ in range(ring[1] - 1):
        yield [pieces[-1]]
        pieces.append(hop(pieces[-1], size, ring))
    return pieces


def slots_of(ring):
    at = position(ring)
    return [(at + ring[1] - back) % ring[1] for back in range(ring[1])]


def join(pieces, ring):
    slots = slots_of(ring)
    ordered = []
    for slot in range(ring[1]):
        chosen = pieces[0]
        for back in range(1, ring[1]):
            chosen = jnp.where(slots[back] == slot, pieces[back], chosen)
        ordered.append(chosen)
    return jnp.concatenate(ordered, axis=0)


def together(one, two):
    results = [None, None]
    live = [one, two]
    while any(g is not None for g in live):
        held = []
        for k, g in enumerate(live):
            if g is None:
                continue
            try:
                held += next(g)
            except StopIteration as stop:
                results[k] = stop.value
                live[k] = None
        if held:
            yield held
    return results


def reduce_over_dp(left, right, size):
    slow, mid, fast = rings(size)
    left, right = yield from together(ring_reduce(left, size, fast), ring_reduce(right, size, mid))
    left, right = yield from together(ring_reduce(left, size, mid), ring_reduce(right, size, fast))
    both = jnp.stack([left, right])
    step = 1
    while step < slow[1]:
        yield [both]
        both = add(lax.ppermute(both, DP, [(i, i ^ (step * slow[0])) for i in range(size)]), both)
        step *= 2
    left, right = yield from together(ring_pieces(both[0], size, mid), ring_pieces(both[1], size, fast))
    left, right = join(left, mid), join(right, fast)
    return (yield from together(ring_pieces(left, size, fast), ring_pieces(right, size, mid)))


def halves_kernel(joins, cuts, at_ref, *refs):
    for side in range(2):
        came, own = refs[2 * side][...], refs[2 * side + 1][...]
        lower = at_ref[side] == 0
        if joins:
            rows = own.shape[0]
            out_ref = refs[4 + side]
            out_ref[:rows] = jnp.where(lower, own, came)
            out_ref[rows:] = jnp.where(lower, came, own)
            continue
        total = (came.astype(F32) + own.astype(F32)).astype(BF16)
        if cuts:
            half = total.shape[0] // 2
            refs[4 + 2 * side][...] = jnp.where(lower, total[half:], total[:half])
            refs[5 + 2 * side][...] = jnp.where(lower, total[:half], total[half:])
        else:
            refs[4 + side][...] = total


def halves(kind, left, right, at, held=()):
    joins, cuts = kind == "join", kind == "cut"
    out_shape = []
    for _, own in (left, right):
        rows, cols = own.shape
        if joins:
            out_shape.append(jax.ShapeDtypeStruct((2 * rows, cols), BF16))
        elif cuts:
            out_shape += [jax.ShapeDtypeStruct((rows // 2, cols), BF16)] * 2
        else:
            out_shape.append(jax.ShapeDtypeStruct((rows, cols), BF16))
    spec = pl.BlockSpec(memory_space=pltpu.VMEM)
    size = left[0].size + right[0].size
    return pl.pallas_call(
        after(functools.partial(halves_kernel, joins, cuts), 5, len(held)),
        in_specs=[pl.BlockSpec(memory_space=pltpu.SMEM)] + [spec] * 4 + [ANY] * len(held),
        out_specs=[spec] * len(out_shape),
        out_shape=out_shape,
        compiler_params=PARAMS,
        cost_estimate=pl.CostEstimate(flops=2 * size, bytes_accessed=8 * size, transcendentals=0),
    )(jnp.stack(at), *left, *right, *held)


def chunk_steps(left, right, rounds, size, calm, wait):
    slow, mid, fast = rings(size)
    at = [position(mid), position(fast)]
    other = [(0, 1), (1, 0)]
    yield [left[0], right[0]]
    came = lax.ppermute(left[0], "fast", other), lax.ppermute(right[0], "mid", other)
    left_away, left_own, right_away, right_own = halves("cut", (came[0], left[1]), (came[1], right[1]), at, rounds.block)
    yield [left_away, right_away]
    came = lax.ppermute(left_away, "mid", other), lax.ppermute(right_away, "fast", other)
    left, right = halves("sum", (came[0], left_own), (came[1], right_own), at, rounds.block)
    if calm:
        yield [left, right]
        left, right = lax.psum((left, right), "slow")
        for _ in range(wait):
            yield []
    else:
        step = 1
        while step < slow[1]:
            yield [left, right]
            hops = [(i, i ^ step) for i in range(slow[1])]
            came = lax.ppermute(left, "slow", hops), lax.ppermute(right, "slow", hops)
            left, right = halves("sum", (came[0], left), (came[1], right), at, rounds.block)
            step *= 2
    yield [left, right]
    came = lax.ppermute(left, "mid", other), lax.ppermute(right, "fast", other)
    left, right = halves("join", (came[0], left), (came[1], right), at, rounds.block)
    yield [left, right]
    return [left, lax.ppermute(left, "fast", other)], [right, lax.ppermute(right, "mid", other)]


def place_kernel(lefts, rights, kept, left_ref, right_ref, *refs):
    pieces, (inner_ref, outer_ref, token_ref) = refs[: lefts + rights], refs[lefts + rights + kept :]
    step = pl.program_id(0)
    for k in range(lefts):

        @pl.when(step == k)
        def _():
            inner_ref[...] = pieces[k][...].astype(F32)

    for k in range(rights):

        @pl.when(step == k)
        def _():
            outer_ref[...] = pieces[lefts + k][...].astype(F32)

    token_ref[...] = jnp.zeros_like(token_ref)


def place(totals, shapes, left, right, fast, mid, at):
    cuts = 2
    steps = max(len(left), len(right))
    rows, cols = left[0].shape
    tall, wide = right[0].shape

    def taken(k, count):
        return lambda j, i, a, b: (jnp.where(j == k, i, jnp.where(j < k, 0, cuts - 1)), 0)

    def last(j, i, count):
        return jnp.minimum(j, count - 1), jnp.where(j < count, i, cuts - 1)

    def left_at(j, i, a, b):
        j, i = last(j, i, len(left))
        return a[j] * cuts + i, at

    def right_at(j, i, a, b):
        j, i = last(j, i, len(right))
        return at * cuts + i, b[j]

    kept = list(totals) if totals else []
    return pl.pallas_call(
        functools.partial(place_kernel, len(left), len(right), len(kept)),
        grid_spec=pltpu.PrefetchScalarGridSpec(
            num_scalar_prefetch=2,
            grid=(steps, cuts),
            in_specs=[pl.BlockSpec((rows // cuts, cols), taken(k, len(left))) for k in range(len(left))]
            + [pl.BlockSpec((tall // cuts, wide), taken(k, len(right))) for k in range(len(right))]
            + [ANY] * len(kept),
            out_specs=[
                pl.BlockSpec((rows // cuts, cols), left_at),
                pl.BlockSpec((tall // cuts, wide), right_at),
                pl.BlockSpec((8, 128), lambda j, i, a, b: (0, 0)),
            ],
        ),
        out_shape=[jax.ShapeDtypeStruct(shape, F32) for shape in shapes] + [jax.ShapeDtypeStruct((8, 128), F32)],
        input_output_aliases={2 + len(left) + len(right) + k: k for k in range(len(kept))},
        compiler_params=PARAMS,
        cost_estimate=pl.CostEstimate(flops=0, bytes_accessed=12 * len(left) * rows * cols, transcendentals=0),
    )(jnp.stack(slots_of(fast)), jnp.stack(slots_of(mid)), *left, *right, *kept)


def butterfly(values, axis, size):
    if size & (size - 1):
        return lax.psum(values, axis)
    step = 1
    while step < size:
        values = values + lax.ppermute(values, axis, [(i, i ^ step) for i in range(size)])
        step *= 2
    return values


class Rounds:
    def __init__(self, finish):
        self.live = []
        self.finish = finish
        self.block = []

    def add(self, at, steps):
        self.live.append((at, steps))

    def turn(self):
        held = self.block
        left = []
        for at, steps in self.live:
            try:
                held = held + next(steps)
                left.append((at, steps))
            except StopIteration as stop:
                held = held + [self.finish(at, *stop.value)]
        self.live = left
        return held


def normalize(values):
    mean_val = jnp.mean(values, axis=-1, keepdims=True)
    centred = values - mean_val
    inv_std = lax.rsqrt(jnp.mean(centred * centred, axis=-1, keepdims=True) + EPSILON)
    return (centred * inv_std, inv_std)


def layout(lengths, row_count):
    slot_count = lengths.shape[0]
    places = jnp.arange(row_count, dtype=jnp.int32)
    seq_ends = jnp.cumsum(lengths)
    seq_starts = seq_ends - lengths
    segment = jnp.sum((places[:, None] >= seq_ends[None, :]).astype(jnp.int32), axis=1)
    member = segment[:, None] == jnp.arange(slot_count, dtype=jnp.int32)[None, :]
    place = places - jnp.sum(jnp.where(member, seq_starts[None, :], 0), axis=1)
    return (segment, place)


def rotary_tables(places):
    half = ROT // 2
    lane = jnp.arange(PAIR, dtype=jnp.int32) % HD
    frequency = jnp.exp(-(2.0 * (lane % half).astype(F32) / ROT) * math.log(10000.0))
    angle = places.astype(F32)[:, None] * jnp.where(lane < ROT, frequency, 0.0)[None, :]
    sign = jnp.where(lane < half, -1.0, jnp.where(lane < ROT, 1.0, 0.0))
    return (jnp.cos(angle), jnp.sin(angle) * sign[None, :])


def local(
    dp_size,
    tensor_size,
    residual,
    norm1_gain,
    norm1_bias,
    norm2_gain,
    norm2_bias,
    qkv_weight,
    qkv_bias,
    dense_weight,
    inner_weight,
    inner_bias,
    outer_weight,
    out_bias,
    cotangent,
    seq_lengths,
):
    width = residual.shape[1]
    head_width = qkv_weight.shape[2]
    hidden = inner_weight.shape[1]
    slots = seq_lengths.shape[1]
    here = lax.axis_index("tensor")
    swap = [(0, 1), (1, 0)]

    if tensor_size == 2:
        other = lax.ppermute(residual, "tensor", swap)
        other_cot = lax.ppermute(cotangent, "tensor", swap)
        parts = (residual, other, cotangent, other_cot)
        order = here
        row_halves = [other, residual]
    else:
        gathered = lax.all_gather(residual, "tensor", axis=0, tiled=True)
        gathered_cot = lax.all_gather(cotangent, "tensor", axis=0, tiled=True)
        middle = gathered.shape[0] // 2
        parts = (gathered[:middle], gathered[middle:], gathered_cot[:middle], gathered_cot[middle:])
        row_halves = list(parts[:2])
        order = jnp.int32(0)
    first_in, second_in, cot = prep(*parts, order, (norm1_gain, norm1_bias, norm2_gain, norm2_bias))
    rows = cot.shape[0]

    _, mid, fast = rings(dp_size)
    short = fast[1] == 2 and mid[1] == 2
    pairs = head_width // PAIR
    totals = []
    arrived = {}

    def finish(at, left, right):
        if isinstance(at, tuple):
            ends = [position(fast), position(mid)]
            arrived[at] = halves("join", left[::-1], right[::-1], ends)
            return arrived[at][0]
        inner, outer, token = place(totals, [(width, hidden), (hidden, width)], left, right, fast, mid, at)
        totals[:] = [inner, outer]
        return token

    rounds = Rounds(finish)
    ffn = {}
    attn = []
    steps = hidden // HIDDEN

    def feed_forward(first, count, calm, wait):
        out = ffn_slice(
            second_in, cot, inner_weight, inner_bias.reshape(1, -1), outer_weight, first, count, fast, mid, rounds.turn()
        )
        rounds.block = [out[2]]
        if short:
            rounds.add(first // count, chunk_steps(out[3], out[4], rounds, dp_size, calm, wait))
        else:
            rounds.add(first // count, reduce_over_dp(out[3], out[4], dp_size))
        ffn[first] = out

    if short and steps % 8 == 0:
        quarter = steps // 4
        feed_forward(2 * quarter, quarter, False, 0)
        feed_forward(0, 2 * quarter, True, 3)
        late = [(3 * quarter, quarter, False, 0)]
    else:
        feed_forward(0, 1, False, 0)
        late = [(k, 1, False, 0) for k in range(1, steps)]
    segment, places = layout(seq_lengths[0], rows)
    cosine, sine = rotary_tables(places)
    qkv = jnp.transpose(qkv_weight, (1, 0, 2))
    chunk = None
    for pair in range(pairs):
        out = attention_pair(
            first_in, cot, qkv, qkv_bias.reshape(3, 1, -1), dense_weight, cosine, sine, segment, slots, pair, fast, mid,
            chunk, pair % CHUNK_PAIRS, rounds.turn(),
        )
        rounds.block = [out[2]]
        attn.append(out)
        chunk = out[3:] if short else None
        if short and (pair % CHUNK_PAIRS == CHUNK_PAIRS - 1 or pair == pairs - 1):
            rounds.add(
                (pair // CHUNK_PAIRS,),
                chunk_steps(tuple(out[3:5]), tuple(out[5:7]), rounds, dp_size, pair < pairs - 1, 2),
            )
            chunk = None
    if not short:
        attn_sums = lax.psum(([a[3] for a in attn], [a[4] for a in attn]), DP)
    for slice_of in late:
        feed_forward(*slice_of)
    ffn = [ffn[first] for first in sorted(ffn)]

    order = here if tensor_size == 2 else jnp.int32(1)
    held = rounds.turn()
    branch_away, branch_own = rows_call(
        functools.partial(branch_kernel, len(attn), len(ffn)), order, [a[0] for a in attn] + [f[0] for f in ffn],
        [dense_weight, outer_weight], [], BF16, 0, held, 2 * rows * width * (head_width + hidden),
    )
    rounds.block = []
    held = rounds.turn() + [branch_away]
    away, own, sums = rows_call(
        functools.partial(back_kernel, len(attn), len(ffn)), order, [a[1] for a in attn] + [f[1] for f in ffn],
        [qkv, inner_weight, norm1_gain.reshape(1, -1), norm2_gain.reshape(1, -1)], row_halves, F32, 4, held,
        2 * rows * width * (3 * head_width + hidden),
    )
    if tensor_size == 2:
        summed = lax.ppermute(branch_away, "tensor", swap).astype(F32) + branch_own.astype(F32)
        combined = lax.ppermute(away, "tensor", swap).astype(F32) + own
    else:
        scatter = functools.partial(lax.psum_scatter, axis_name="tensor", scatter_dimension=0, tiled=True)
        summed = scatter(jnp.concatenate([branch_away, branch_own], axis=0)).astype(F32)
        combined = scatter(jnp.concatenate([away.astype(F32), own], axis=0))
    layer_out = (residual.astype(F32) + summed + out_bias).astype(BF16)
    own_normed, own_inv = normalize(residual.astype(F32))
    residual_grad = (
        cotangent.astype(F32)
        + own_inv
        * (
            combined
            - jnp.mean(combined, axis=-1, keepdims=True)
            - own_normed * jnp.mean(combined * own_normed, axis=-1, keepdims=True)
        )
    ).astype(BF16)

    over_all = jnp.concatenate([sums, jnp.sum(cotangent.astype(F32), axis=0, keepdims=True)], axis=0).reshape(-1)
    over_all = butterfly(over_all, "tensor", tensor_size)
    qkvbias = jnp.concatenate([a[2].reshape(3, PAIR) for a in attn], axis=1).reshape(-1)
    innerbias = jnp.concatenate([f[2] for f in ffn], axis=1).reshape(-1)
    vectors = butterfly(jnp.concatenate([over_all, qkvbias, innerbias]), DP, dp_size)
    ends = [width * i for i in range(1, 6)] + [5 * width + 3 * head_width]
    gain1_grad, bias1_grad, gain2_grad, bias2_grad, outbias_grad, qkvbias_grad, innerbias_grad = jnp.split(vectors, ends)

    rounds.block = []
    while rounds.live:
        rounds.turn()
    inner_grad, outer_grad = totals
    if short:
        lefts = [arrived[key][0].reshape(width, CHUNK_PAIRS, 2, PAIR) for key in sorted(arrived)]
        rights = [arrived[key][1].reshape(width, CHUNK_PAIRS, 2, PAIR) for key in sorted(arrived)]
        both = jnp.concatenate(lefts, axis=1)[:, :pairs].transpose(0, 2, 1, 3).reshape(width, 2, head_width)
        rest = jnp.concatenate(rights, axis=1)[:, :pairs].transpose(0, 2, 1, 3).reshape(width, 2, head_width)
        qkv_grad = jnp.concatenate([both, rest[:, :1]], axis=1).astype(F32)
        dense_grad = rest[:, 1].reshape(width // PAIR, PAIR, head_width // PAIR, PAIR).transpose(2, 1, 0, 3)
        dense_grad = dense_grad.reshape(head_width, width).astype(F32)
    else:
        qkv_sums, dense_sums = attn_sums
        qkv_grad = jnp.concatenate([g.transpose(1, 0, 2) for g in qkv_sums], axis=2).astype(F32)
        dense_grad = jnp.concatenate(dense_sums, axis=0).astype(F32)
    return (
        layer_out,
        residual_grad,
        gain1_grad,
        bias1_grad,
        gain2_grad,
        bias2_grad,
        qkv_grad,
        qkvbias_grad.reshape(3, head_width),
        dense_grad,
        inner_grad,
        innerbias_grad,
        outer_grad,
        outbias_grad,
    )


def solution(mesh):
    dp_size, tensor_size = mesh.shape["dp"], mesh.shape["tensor"]
    digits = [length for _, length in rings(dp_size)]
    rows = P(DP + ("tensor",), None)
    return jax.shard_map(
        functools.partial(local, dp_size, tensor_size),
        mesh=Mesh(mesh.devices.reshape(*digits, tensor_size), DP + ("tensor",)),
        in_specs=(
            rows,
            P(),
            P(),
            P(),
            P(),
            P(None, None, "tensor"),
            P(None, "tensor"),
            P("tensor", None),
            P(None, "tensor"),
            P("tensor"),
            P("tensor", None),
            P(),
            rows,
            P(DP, None),
        ),
        out_specs=(
            rows,
            rows,
            P(),
            P(),
            P(),
            P(),
            P(None, None, "tensor"),
            P(None, "tensor"),
            P("tensor", None),
            P(None, "tensor"),
            P("tensor"),
            P("tensor", None),
            P(),
        ),
        check_vma=False,
    )
```
